32 devices in a mesh: groups: 2 (over y), ctx: 4 (over x, core), chan: 4 (over z).
Axes of the slice: x: 2, y: 2, z: 4, core: 2. Of those that a mesh axis runs over, the one named last changes fastest.
Arguments:
- stream: bfloat16 [1536, 4096], P(('groups', 'ctx'), 'chan'), parts along dimension 0, may hold values from -30 to 30
- in_weights: bfloat16 [2, 4096, 3, 2048], P(None, 'ctx', None, 'chan'), may hold values from -0.09375 to 0.09375
- out_weights: bfloat16 [2, 4096, 2048], P(None, 'ctx', 'chan'), may hold values from -0.125 to 0.125
- short_taps: bfloat16 [7, 2048], P(None, 'chan'), may hold values from -2.390625 to 2.390625
- medium_taps: bfloat16 [128, 128], P(None, 'chan'), may hold values from -0.5390625 to 0.5390625
- plan: int32 [4], replicated, may hold values from 0 to 1
Outputs:
- result: bfloat16 [1536, 4096], P(('groups', 'ctx'), 'chan'), parts along dimension 0
The draws below stay inside these ranges and needn't reach their ends.
There are 2 independent parts, one for each index of `groups`. The reference program is written for one: setup_inputs(seed, part) draws one part's arguments, and reference() takes and returns one part's arrays. A program takes and returns all parts, laid end to end along the dimension named above; an argument that names none is the same for every part. Nothing has to cross between parts.
All inputs are finite; a program needn't handle non-finite values.
Results may differ from the reference program's by a relative error of at most 0.03.
Values may be sent and summed in bfloat16 or wider, within the bound.
No kernel may reach another device: no remote copies, remote signals or barrier semaphores. Data moves between devices by JAX's collectives and lax.ppermute only.
A program may use at most 128 MiB of HBM per device.

```python
import jax
import jax.numpy as jnp
from jax import lax

D = 4096
C = 2048
SHORT_TAPS = 7
MEDIUM_TAPS = 128
STEPS = 4
TOKENS = 768
GROUPS = 128
N_CHAN = 4


def draw_stream(key, part):
    key_list = jax.random.split(key, 4)
    row_scale = jnp.exp(jax.random.uniform(key_list[0], (TOKENS, 1), jnp.float32, jnp.log(0.3), jnp.log(3.0)))
    col_scale = jnp.exp(jax.random.uniform(key_list[1], (1, D), jnp.float32, jnp.log(0.3), jnp.log(3.0)))
    base_noise = jax.random.truncated_normal(key_list[3], -4.0, 4.0, (TOKENS, D), jnp.float32)
    return jnp.clip(base_noise * row_scale * col_scale, -30.0, 30.0).astype(jnp.bfloat16)


def with_ends(drawn, rng, low, high):
    place = [jax.random.randint(jax.random.fold_in(rng, axis), (), 0, length) for axis, length in enumerate(drawn.shape)]
    main_axis = drawn.shape.index(max(drawn.shape))
    beside = place[:main_axis] + [(place[main_axis] + 1) % drawn.shape[main_axis]] + place[main_axis + 1:]
    return drawn.at[tuple(place)].set(low).at[tuple(beside)].set(high)


def block_scale(stream_key, dims, shards, low, top_value):
    def one(dim, parts):
        heights = jax.random.uniform(jax.random.fold_in(jax.random.fold_in(stream_key, 6), dim), (parts,), jnp.float32, low / len(shards), top_value / len(shards))
        return jnp.repeat(jnp.exp(heights), dims[dim] // parts).reshape((-1,) + (1,) * (len(dims) - dim - 1))

    level = one(*shards[0])
    for cut in shards[1:]:
        level = level * one(*cut)
    return level


def bell_draw(key, extent, width, limit, pieces=(), kind=jnp.bfloat16):
    entries = jax.random.normal(key, extent, jnp.float32) * width
    if len(pieces) > 0:
        entries = block_scale(key, extent, pieces, -0.22, 0.18) * entries
    return jnp.clip(entries, min=-limit, max=limit).astype(kind)


def setup_inputs(seed: int = 0, part: int = 0) -> dict:
    seeds = jax.random.split(jax.random.key(seed), 7)
    own_keys = jax.random.split(jax.random.fold_in(seeds[6], part), 7)
    stream = draw_stream(jax.random.fold_in(jax.random.fold_in(seeds[6], part), 71), part)
    in_weights = bell_draw(seeds[1], (2, D, 3, C), D ** -0.5, 0.09375, ((1, 4), (3, 4)))
    out_weights = bell_draw(seeds[2], (2, D, C), C ** -0.5, 0.125, ((1, 4), (2, 4)))
    short_taps = bell_draw(seeds[3], (SHORT_TAPS, C), 0.4, 2.390625, ((1, 4),))
    medium_taps = bell_draw(seeds[4], (MEDIUM_TAPS, GROUPS), 0.09, 0.5390625, ((1, 4),))
    plan = with_ends(jax.random.randint(seeds[5], (STEPS,), 0, 2), jax.random.fold_in(seeds[5], 1), 0, 1).astype(jnp.int32)
    return {"stream": stream, "in_weights": in_weights, "out_weights": out_weights, "short_taps": short_taps, "medium_taps": medium_taps, "plan": plan}


def section_taps(section, short_taps, medium_taps):
    reach = medium_taps.shape[0]
    channels = short_taps.shape[1]
    padding = jnp.zeros((reach - short_taps.shape[0], channels), short_taps.dtype)
    short_full = jnp.concatenate([short_taps, padding], 0)
    group_size = channels // medium_taps.shape[1]
    medium_full = jnp.broadcast_to(medium_taps[:, :, None], (reach, medium_taps.shape[1], group_size)).reshape(reach, channels)
    return jnp.where(section == 0, short_full, medium_full)

def causal_filter(extended, filter_taps):
    reach = filter_taps.shape[0]
    length = extended.shape[0] - reach + 1
    taps_wide = filter_taps.astype(jnp.float32)

    def add_tap(tap_index, total):
        index_now = jnp.asarray(tap_index).astype(jnp.int32)
        start = (jnp.int32(reach - 1) - index_now).astype(jnp.int32)
        window = lax.dynamic_slice_in_dim(extended, start, length, 0).astype(jnp.float32)
        weight_row = lax.dynamic_index_in_dim(taps_wide, index_now, 0, keepdims=True)
        return total + weight_row * window
    start_total = jnp.zeros((length, extended.shape[1]), jnp.float32)
    return lax.fori_loop(0, reach, add_tap, start_total)

def reference(stream, in_weights, out_weights, short_taps, medium_taps, plan):
    hidden = stream
    tokens = stream.shape[0]
    block_width = C // N_CHAN
    for step_index in range(STEPS):
        section = plan[step_index]
        weight_in = lax.dynamic_index_in_dim(in_weights, section, 0, keepdims=False)
        weight_out = lax.dynamic_index_in_dim(out_weights, section, 0, keepdims=False)
        widened = hidden.astype(jnp.float32)
        row_scale = lax.rsqrt(lax.optimization_barrier(jnp.mean(widened * widened, axis=1, keepdims=True)) + 1e-05)
        projected = jnp.dot(hidden, weight_in.reshape(D, 3 * C), preferred_element_type=jnp.float32)
        projected = projected.reshape(tokens, 3, C) * row_scale[:, :, None]
        query_bf = projected[:, 0].astype(jnp.bfloat16)
        mixed_bf = (projected[:, 1] * projected[:, 2]).astype(jnp.bfloat16)
        history = jnp.zeros((MEDIUM_TAPS - 1, C), jnp.bfloat16)
        filtered = causal_filter(jnp.concatenate([history, mixed_bf], 0), section_taps(section, short_taps, medium_taps))
        gated_bf = (query_bf.astype(jnp.float32) * filtered).astype(jnp.bfloat16)
        update = jnp.zeros((tokens, D), jnp.float32)
        for block_index in range(N_CHAN):
            lower = block_index * block_width
            block_term = lax.dot_general(gated_bf[:, lower:lower + block_width], weight_out[:, lower:lower + block_width], (((1,), (1,)), ((), ())), preferred_element_type=jnp.float32)
            update = update + lax.optimization_barrier(block_term.astype(jnp.bfloat16)).astype(jnp.float32)
        hidden = (hidden.astype(jnp.float32) + update).astype(jnp.bfloat16)
    return hidden
```

```python
from functools import partial

import jax
import jax.numpy as jnp
from jax import lax
from jax.experimental import pallas as pl
from jax.experimental.pallas import tpu as pltpu
from jax.sharding import PartitionSpec as P

STEPS = 4
VMEM_BYTES = 48 * 1024 * 1024


def passed_along(value, axis, steps):
    count = lax.axis_size(axis)
    leading, last = (max(0, -steps), min(count, count - steps))
    return lax.ppermute(value, axis, [(source, source + steps) for source in range(leading, last)])


def section_taps(section, short_taps, medium_taps):
    reach = medium_taps.shape[0]
    channels = short_taps.shape[1]
    padding = jnp.zeros((reach - short_taps.shape[0], channels), short_taps.dtype)
    short_full = jnp.concatenate([short_taps, padding], 0)
    group_size = channels // medium_taps.shape[1]
    medium_full = jnp.broadcast_to(
        medium_taps[:, :, None], (reach, medium_taps.shape[1], group_size)
    ).reshape(reach, channels)
    return jnp.where(section == 0, short_full, medium_full)


def causal_filter(extended, filter_taps):
    filtered = lax.conv_general_dilated(
        extended[None],
        filter_taps[::-1][:, None, :],
        (1,),
        "VALID",
        dimension_numbers=("NWC", "WIO", "NWC"),
        feature_group_count=filter_taps.shape[1],
        preferred_element_type=jnp.float32,
    )
    return filtered[0]


def filter_gate(projected, section, short_taps, medium_taps):
    query_bf = projected[:, 0].astype(jnp.bfloat16)
    mixed_bf = (projected[:, 1] * projected[:, 2]).astype(jnp.bfloat16)
    reach = medium_taps.shape[0]
    earlier = passed_along(mixed_bf[-reach:], "ctx", 1)
    extended = jnp.concatenate([earlier[1:], mixed_bf], 0)
    filtered = causal_filter(extended, section_taps(section, short_taps, medium_taps))
    return (query_bf.astype(jnp.float32) * filtered).astype(jnp.bfloat16)


def general_shards(stream, in_weights, out_weights, short_taps, medium_taps, plan):
    hidden = stream
    weights_in = lax.all_gather(in_weights, "ctx", axis=1, tiled=True)
    weights_out = lax.all_gather(out_weights, "ctx", axis=1, tiled=True)
    for step in range(STEPS):
        section = plan[step]
        full_rows = lax.all_gather(hidden, "chan", axis=1, tiled=True)
        widened = full_rows.astype(jnp.float32)
        row_scale = lax.rsqrt(jnp.mean(widened * widened, axis=1, keepdims=True) + 1e-05)
        chosen = lax.dynamic_index_in_dim(weights_in, section, 0, keepdims=False)
        projected = jnp.dot(
            full_rows, chosen.reshape(chosen.shape[0], -1), preferred_element_type=jnp.float32
        )
        projected = projected.reshape(full_rows.shape[0], 3, -1) * row_scale[:, :, None]
        gated = filter_gate(projected, section, short_taps, medium_taps)
        chosen = lax.dynamic_index_in_dim(weights_out, section, 0, keepdims=False)
        product = lax.dot_general(
            gated, chosen, (((1,), (1,)), ((), ())), preferred_element_type=jnp.float32
        )
        update = lax.psum_scatter(
            product.astype(jnp.bfloat16), "chan", scatter_dimension=1, tiled=True
        ).astype(jnp.float32)
        hidden = (hidden.astype(jnp.float32) + update).astype(jnp.bfloat16)
    return hidden


SECOND, GROUP, SAME, ROW_OWN, ROW_CORE, ROW_CHIP, ROW_BOTH, HELD = range(8)


def ctx_pairs(change):
    return [(i, i ^ change) for i in range(4)]


def flat(i, j, g=None):
    return (i * 4 + j) if g is None else (g * 16 + i * 4 + j)


def in_kernel(sections, meta, *refs):
    pieces = refs[:4]
    weights = [refs[4 + 18 * s : 4 + 18 * (s + 1)] for s in range(sections)]
    query_ref, mixed_ref = refs[4 + 18 * sections : 6 + 18 * sections]
    hidden, held, total, hidden_sem, held_sem = refs[6 + 18 * sections :]
    width = hidden.shape[2]
    part = width // 2
    group = meta[GROUP]

    hidden_copies = [
        pltpu.make_async_copy(pieces[k], hidden.at[meta[HELD + k]], hidden_sem.at[k])
        for k in range(4)
    ]
    for copy in hidden_copies:
        copy.start()

    def copies(refs_s):
        out = []
        for p in range(3):
            own, core, chip, chip_y, both, both_y = refs_s[6 * p : 6 * p + 6]
            mine = pl.ds(pl.multiple_of(group * part, part), part)
            other = pl.ds(pl.multiple_of((1 - group) * part, part), part)
            out.append(
                [
                    pltpu.make_async_copy(own, held.at[p, 0], held_sem.at[p, 0]),
                    pltpu.make_async_copy(core, held.at[p, 1], held_sem.at[p, 1]),
                    pltpu.make_async_copy(chip, held.at[p, 2, mine], held_sem.at[p, 2]),
                    pltpu.make_async_copy(chip_y, held.at[p, 2, other], held_sem.at[p, 3]),
                    pltpu.make_async_copy(both, held.at[p, 3, mine], held_sem.at[p, 4]),
                    pltpu.make_async_copy(both_y, held.at[p, 3, other], held_sem.at[p, 5]),
                ]
            )
        return out

    def start(refs_s):
        for per in copies(refs_s):
            for copy in per:
                copy.start()

    if sections == 1:
        start(weights[0])
    else:
        pl.when(meta[SECOND] == 0)(lambda: start(weights[0]))
        pl.when(meta[SECOND] != 0)(lambda: start(weights[1]))
    waits = copies(weights[0])

    for copy in hidden_copies:
        copy.wait()
    square = jnp.zeros((hidden.shape[1], 1), jnp.float32)
    for k in range(4):
        wide = hidden[k].astype(jnp.float32)
        square = square + jnp.sum(wide * wide, axis=1, keepdims=True)
    scale = lax.rsqrt(square / (4 * width) + 1e-05)

    rows = (ROW_OWN, ROW_CORE, ROW_CHIP, ROW_BOTH)
    spans = ((0,), (1,), (2, 3), (4, 5))
    for p in range(3):
        for r in range(4):
            for s in spans[r]:
                waits[p][s].wait()
            product = jnp.dot(
                hidden[meta[rows[r]]], held[p, r], preferred_element_type=jnp.float32
            )
            if r == 0:
                total[p] = product
            else:
                total[p] += product
    query_ref[...] = (total[0] * scale).astype(query_ref.dtype)
    mixed_ref[...] = ((total[1] * scale) * (total[2] * scale)).astype(mixed_ref.dtype)


def project_in(meta, pieces, weights):
    tokens, width = pieces[0].shape
    channels = weights[0][0].shape[1]
    sections = len(weights)
    anywhere = pl.BlockSpec(memory_space=pl.ANY)
    vmem = pl.BlockSpec(memory_space=pltpu.VMEM)
    out = jax.ShapeDtypeStruct((tokens, channels), jnp.bfloat16)
    return pl.pallas_call(
        partial(in_kernel, sections),
        out_shape=(out, out),
        in_specs=[pl.BlockSpec(memory_space=pltpu.SMEM)] + [anywhere] * (4 + 18 * sections),
        out_specs=(vmem, vmem),
        scratch_shapes=[
            pltpu.VMEM((4, tokens, width), jnp.bfloat16),
            pltpu.VMEM((3, 4, width, channels), jnp.bfloat16),
            pltpu.VMEM((3, tokens, channels), jnp.float32),
            pltpu.SemaphoreType.DMA((4,)),
            pltpu.SemaphoreType.DMA((3, 6)),
        ],
        compiler_params=pltpu.CompilerParams(vmem_limit_bytes=VMEM_BYTES),
        cost_estimate=pl.CostEstimate(
            flops=24 * tokens * width * channels,
            bytes_accessed=24 * width * channels,
            transcendentals=0,
        ),
        name="project_in",
    )(meta, *pieces, *[w for ws in weights for w in ws])


BLOCK = 64


def filter_kernel(meta, halo, mixed, query, bands, short, gated, extended):
    reach, tokens = halo.shape[0], mixed.shape[0]
    channels = mixed.shape[1]
    group_size = channels // (bands.shape[0] // BLOCK)

    @pl.when(meta[0] == 0)
    def _():
        extended[:reach] = halo[...].astype(jnp.float32)
        extended[reach:] = mixed[...].astype(jnp.float32)
        taps = short[...].astype(jnp.float32)
        total = jnp.zeros((tokens, channels), jnp.float32)
        for t in range(taps.shape[0]):
            total = total + taps[t : t + 1] * extended[reach - t : reach - t + tokens]
        gated[...] = (query[...].astype(jnp.float32) * total).astype(gated.dtype)

    @pl.when(meta[0] != 0)
    def _():
        lanes = 128
        per_tile = lanes // group_size
        lane_group = lax.broadcasted_iota(jnp.int32, (BLOCK, lanes), 1) // group_size
        for tile in range(channels // lanes):
            at = slice(tile * lanes, (tile + 1) * lanes)
            column = jnp.concatenate([halo[:, at], mixed[:, at]], 0)
            band = bands[tile * per_tile * BLOCK : (tile + 1) * per_tile * BLOCK]
            for b in range(tokens // BLOCK):
                window = column[b * BLOCK : b * BLOCK + reach + BLOCK]
                product = jnp.dot(band, window, preferred_element_type=jnp.float32)
                total = product[:BLOCK]
                for m in range(1, per_tile):
                    total = jnp.where(
                        lane_group == m, product[m * BLOCK : (m + 1) * BLOCK], total
                    )
                rows = slice(b * BLOCK, (b + 1) * BLOCK)
                gated[rows, at] = (query[rows, at].astype(jnp.float32) * total).astype(gated.dtype)


def filter_and_gate(section, halo, mixed, query, bands, short):
    tokens, channels = mixed.shape
    vmem = pl.BlockSpec(memory_space=pltpu.VMEM)
    return pl.pallas_call(
        filter_kernel,
        out_shape=jax.ShapeDtypeStruct(mixed.shape, jnp.bfloat16),
        in_specs=[pl.BlockSpec(memory_space=pltpu.SMEM)] + [vmem] * 5,
        out_specs=vmem,
        scratch_shapes=[pltpu.VMEM((halo.shape[0] + tokens, channels), jnp.float32)],
        compiler_params=pltpu.CompilerParams(vmem_limit_bytes=VMEM_BYTES),
        cost_estimate=pl.CostEstimate(
            flops=2 * tokens * channels * 1024, bytes_accessed=8 * tokens * channels, transcendentals=0
        ),
        name="filter_and_gate",
    )(section.reshape(1), halo, mixed, query, bands, short)


def tap_bands(medium_taps):
    reach, groups = medium_taps.shape
    length = 2 * reach
    zero = jnp.zeros((groups, 1), medium_taps.dtype)
    tail = jnp.zeros((groups, reach - 1), medium_taps.dtype)
    cycle = jnp.concatenate([zero, medium_taps[::-1].T, tail], 1)
    skewed = jnp.broadcast_to(cycle[:, None], (groups, BLOCK, length)).reshape(groups, -1)
    skewed = skewed[:, : BLOCK * (length - 1)].reshape(groups, BLOCK, length - 1)
    return skewed[:, :, : reach + BLOCK].reshape(groups * BLOCK, reach + BLOCK)


def out_kernel(sections, meta, *refs):
    own_gated, core_gated = refs[:4], refs[4:8]
    own_hidden, core_hidden = refs[8:10]
    weights = [refs[10 + 16 * s : 10 + 16 * (s + 1)] for s in range(sections)]
    own_out, core_out, held, held_sem = refs[10 + 16 * sections :]
    tokens, width = own_hidden.shape
    part = width // 2
    group = meta[GROUP]
    mine = pl.ds(pl.multiple_of(group * part, part), part)
    other = pl.ds(pl.multiple_of((1 - group) * part, part), part)

    def start(sources):
        for k in range(4):
            pltpu.make_async_copy(sources[2 * k], held.at[k, mine], held_sem.at[k, 0]).start()
            pltpu.make_async_copy(sources[2 * k + 1], held.at[k, other], held_sem.at[k, 1]).start()

    for s in range(sections):
        for same in range(2):
            here = meta[SAME] == same
            if sections > 1:
                here = jnp.logical_and(here, meta[SECOND] == s)
            pl.when(here)(partial(start, weights[s][8 * (1 - same) : 8 * (1 - same) + 8]))

    total = None
    for k in range(4):
        pltpu.make_async_copy(weights[0][2 * k], held.at[k, mine], held_sem.at[k, 0]).wait()
        pltpu.make_async_copy(weights[0][2 * k + 1], held.at[k, other], held_sem.at[k, 1]).wait()
        both = jnp.concatenate([own_gated[k][...], core_gated[k][...]], 0)
        product = lax.dot_general(
            both, held[k], (((1,), (1,)), ((), ())), preferred_element_type=jnp.float32
        )
        total = product if total is None else total + product
    own_out[...] = (own_hidden[...].astype(jnp.float32) + total[:tokens]).astype(own_out.dtype)
    core_out[...] = (core_hidden[...].astype(jnp.float32) + total[tokens:]).astype(core_out.dtype)


def project_out(meta, own_gated, core_gated, own_hidden, core_hidden, weights):
    tokens, width = own_hidden.shape
    channels = own_gated[0].shape[1]
    sections = len(weights)
    anywhere = pl.BlockSpec(memory_space=pl.ANY)
    vmem = pl.BlockSpec(memory_space=pltpu.VMEM)
    out = jax.ShapeDtypeStruct((tokens, width), jnp.bfloat16)
    return pl.pallas_call(
        partial(out_kernel, sections),
        out_shape=(out, out),
        in_specs=[pl.BlockSpec(memory_space=pltpu.SMEM)] + [vmem] * 10 + [anywhere] * (16 * sections),
        out_specs=(vmem, vmem),
        scratch_shapes=[
            pltpu.VMEM((4, width, channels), jnp.bfloat16),
            pltpu.SemaphoreType.DMA((4, 2)),
        ],
        compiler_params=pltpu.CompilerParams(vmem_limit_bytes=VMEM_BYTES),
        cost_estimate=pl.CostEstimate(
            flops=16 * tokens * width * channels,
            bytes_accessed=8 * width * channels,
            transcendentals=0,
        ),
        name="project_out",
    )(meta, *own_gated, *core_gated, own_hidden, core_hidden, *[w for ws in weights for w in ws])


def gathered_in(in_weights, section, g):
    chosen = lax.dynamic_index_in_dim(in_weights, section, 0, keepdims=False)
    part = chosen.shape[0] // 2
    pieces = [None] * 3
    for p in (1, 2, 0):
        own = chosen[:, p]
        half = lax.dynamic_slice_in_dim(own, g * part, part, 0)
        chip = lax.ppermute(half, "ctx", ctx_pairs(2))
        chip_y = lax.ppermute(chip, "groups", [(0, 1), (1, 0)])
        core = lax.ppermute(own, "ctx", ctx_pairs(1))
        both = lax.ppermute(chip, "ctx", ctx_pairs(1))
        both_y = lax.ppermute(chip_y, "ctx", ctx_pairs(1))
        pieces[p] = [own, core, chip, chip_y, both, both_y]
    return [a for per in pieces for a in per]


def gathered_out(out_weights, section, g):
    shard = lax.dynamic_index_in_dim(out_weights, section, 0, keepdims=False)
    part = shard.shape[0] // 2
    half = lax.dynamic_slice_in_dim(shard, g * part, part, 0)
    rest = lax.dynamic_slice_in_dim(shard, (1 - g) * part, part, 0)
    axes = ("ctx", "chan")
    every = ("groups", "ctx", "chan")

    def along(k):
        return [
            (flat(2 * x + (j % 2), (j - k) % 4), flat(3 * x, j)) for x in range(2) for j in range(4)
        ]

    across = [(flat(3 * x, j), flat(2 * (1 - x) + x, j)) for x in range(2) for j in range(4)]
    swap_same = [
        (flat(3 * x, j, q), flat(3 * x, j, 1 - q)) for x in range(2) for j in range(4) for q in range(2)
    ]
    swap_cross = [
        (flat(2 * (1 - x) + x, j, q), flat(2 * (1 - x) + x, j, 1 - q))
        for x in range(2)
        for j in range(4)
        for q in range(2)
    ]
    same, cross = [], []
    for k in range(4):
        mine = lax.ppermute(half, axes, along(k))
        if k == 0:
            other = lax.ppermute(rest, axes, along(k))
        else:
            other = lax.ppermute(mine, every, swap_same)
        sent = lax.ppermute(mine, axes, across)
        sent_y = lax.ppermute(sent, every, swap_cross)
        same += [mine, other]
        cross += [sent, sent_y]
    return same + cross


def shards(stream, in_weights, out_weights, short_taps, medium_taps, plan):
    g, i, j = lax.axis_index("groups"), lax.axis_index("ctx"), lax.axis_index("chan")
    x, c, h = i // 2, i % 2, j % 2
    first = plan[0]
    sections = (first, 1 - first)
    reach = medium_taps.shape[0]
    bands = tap_bands(medium_taps)

    slots = [stream] + [
        lax.ppermute(stream, "chan", [(s, (s + k) % 4) for s in range(4)]) for k in (1, 2, 3)
    ]
    held = [(j - k) % 4 for k in range(4)]
    near = (j // 2) == c
    own_hidden = jnp.where(near, slots[0], slots[2])
    core_hidden = lax.ppermute(jnp.where(near, slots[2], slots[0]), "ctx", ctx_pairs(1))

    weights_in = [gathered_in(in_weights, sections[0], g)]
    weights_out = [gathered_out(out_weights, sections[0], g)]
    weights_in.append(gathered_in(in_weights, sections[1], g))
    weights_out.append(gathered_out(out_weights, sections[1], g))

    for step in range(STEPS):
        count = 1 if step == 0 else 2
        section = plan[step]
        second = (section != first).astype(jnp.int32)
        scalars = [second, g, (x == c).astype(jnp.int32), i, i ^ 1, i ^ 2, i ^ 3] + held
        meta = jnp.stack([jnp.asarray(s, jnp.int32) for s in scalars])
        query, mixed = project_in(meta, slots, weights_in[:count])
        halo = lax.ppermute(mixed[-reach:], "ctx", [(0, 1), (1, 2), (2, 3)])
        gated = filter_and_gate(section, halo, mixed, query, bands, short_taps)
        own_gated = [gated] + [
            lax.ppermute(gated, "chan", [(s, (s + k) % 4) for s in range(4)]) for k in (1, 2, 3)
        ]
        core_gated = [lax.ppermute(a, "ctx", ctx_pairs(1)) for a in own_gated]
        own_hidden, core_hidden = project_out(
            meta, own_gated, core_gated, own_hidden, core_hidden, weights_out[:count]
        )
        swapped = lax.ppermute(core_hidden, "ctx", ctx_pairs(1))
        beside = [(s, s ^ 1) for s in range(4)]
        if step < STEPS - 1:
            slots = [own_hidden, swapped] + [
                lax.ppermute(a, "chan", beside) for a in (own_hidden, swapped)
            ]
            held = [2 * c + h, 2 * (1 - c) + h, 2 * c + 1 - h, 2 * (1 - c) + 1 - h]
    return jnp.where(near, own_hidden, swapped)


def solution(mesh):
    special = dict(mesh.shape) == {"groups": 2, "ctx": 4, "chan": 4}
    return jax.shard_map(
        shards if special else general_shards,
        mesh=mesh,
        in_specs=(
            P(("groups", "ctx"), "chan"),
            P(None, "ctx", None, "chan"),
            P(None, "ctx", "chan"),
            P(None, "chan"),
            P(None, "chan"),
            P(),
        ),
        out_specs=P(("groups", "ctx"), "chan"),
        check_vma=False,
    )
```

```python
from functools import partial

import jax
import jax.numpy as jnp
from jax import lax
from jax.experimental import pallas as pl
from jax.experimental.pallas import tpu as pltpu
from jax.sharding import PartitionSpec as P

STEPS = 4
MIB = 1024 * 1024


def passed_along(value, axis, steps):
    count = lax.axis_size(axis)
    leading, last = (max(0, -steps), min(count, count - steps))
    return lax.ppermute(value, axis, [(source, source + steps) for source in range(leading, last)])


def section_taps(section, short_taps, medium_taps):
    reach = medium_taps.shape[0]
    channels = short_taps.shape[1]
    padding = jnp.zeros((reach - short_taps.shape[0], channels), short_taps.dtype)
    short_full = jnp.concatenate([short_taps, padding], 0)
    group_size = channels // medium_taps.shape[1]
    medium_full = jnp.broadcast_to(
        medium_taps[:, :, None], (reach, medium_taps.shape[1], group_size)
    ).reshape(reach, channels)
    return jnp.where(section == 0, short_full, medium_full)


def causal_filter(extended, filter_taps):
    filtered = lax.conv_general_dilated(
        extended[None],
        filter_taps[::-1][:, None, :],
        (1,),
        "VALID",
        dimension_numbers=("NWC", "WIO", "NWC"),
        feature_group_count=filter_taps.shape[1],
        preferred_element_type=jnp.float32,
    )
    return filtered[0]


def filter_gate(projected, section, short_taps, medium_taps):
    query_bf = projected[:, 0].astype(jnp.bfloat16)
    mixed_bf = (projected[:, 1] * projected[:, 2]).astype(jnp.bfloat16)
    reach = medium_taps.shape[0]
    earlier = passed_along(mixed_bf[-reach:], "ctx", 1)
    extended = jnp.concatenate([earlier[1:], mixed_bf], 0)
    filtered = causal_filter(extended, section_taps(section, short_taps, medium_taps))
    return (query_bf.astype(jnp.float32) * filtered).astype(jnp.bfloat16)


def general_shards(stream, in_weights, out_weights, short_taps, medium_taps, plan):
    hidden = stream
    weights_in = lax.all_gather(in_weights, "ctx", axis=1, tiled=True)
    weights_out = lax.all_gather(out_weights, "ctx", axis=1, tiled=True)
    for step in range(STEPS):
        section = plan[step]
        full_rows = lax.all_gather(hidden, "chan", axis=1, tiled=True)
        widened = full_rows.astype(jnp.float32)
        row_scale = lax.rsqrt(jnp.mean(widened * widened, axis=1, keepdims=True) + 1e-05)
        chosen = lax.dynamic_index_in_dim(weights_in, section, 0, keepdims=False)
        projected = jnp.dot(
            full_rows, chosen.reshape(chosen.shape[0], -1), preferred_element_type=jnp.float32
        )
        projected = projected.reshape(full_rows.shape[0], 3, -1) * row_scale[:, :, None]
        gated = filter_gate(projected, section, short_taps, medium_taps)
        chosen = lax.dynamic_index_in_dim(weights_out, section, 0, keepdims=False)
        product = lax.dot_general(
            gated, chosen, (((1,), (1,)), ((), ())), preferred_element_type=jnp.float32
        )
        update = lax.psum_scatter(
            product.astype(jnp.bfloat16), "chan", scatter_dimension=1, tiled=True
        ).astype(jnp.float32)
        hidden = (hidden.astype(jnp.float32) + update).astype(jnp.bfloat16)
    return hidden


SECOND, GROUP, SAME, ROW_OWN, ROW_CORE, ROW_CHIP, ROW_BOTH, HELD = range(8)


def ctx_pairs(change):
    return [(i, i ^ change) for i in range(4)]


def flat(i, j, g=None):
    return (i * 4 + j) if g is None else (g * 16 + i * 4 + j)


def in_kernel(sections, meta, section_ref, *refs):
    count = 1 if sections == 1 else 4
    pieces, refs = refs[:count], refs[count:]
    own_in, core_in = refs[:2]
    weights = [refs[2 + 6 * s : 8 + 6 * s] for s in range(sections)]
    query_ref, mixed_ref, hidden, held, total, held_sem = refs[2 + 6 * sections :]
    width = hidden.shape[2]
    part = width // 2
    group = meta[GROUP]
    section = section_ref[0]
    rows = (ROW_OWN, ROW_CORE, ROW_CHIP, ROW_BOTH)

    def span(q):
        return pl.ds(pl.multiple_of(q * part, part), part)

    def start(p, r, source, at, q):
        pltpu.make_async_copy(source, held.at[p, r, at], held_sem.at[p, r, q]).start()

    def start_section(chip, chip_y, both, both_y, chip_q, both_q):
        for p in (1, 2, 0):
            for q in range(2):
                start(p, 0, own_in.at[section, p, span(q)], span(q), q)
                start(p, 1, core_in.at[section, p, span(q)], span(q), q)
                if p == 0:
                    start(p, 2, chip_q.at[span(q)], span(q), q)
                    start(p, 3, both_q.at[span(q)], span(q), q)
            if p > 0:
                start(p, 2, chip.at[p - 1], span(group), 0)
                start(p, 2, chip_y.at[p - 1], span(1 - group), 1)
                start(p, 3, both.at[p - 1], span(group), 0)
                start(p, 3, both_y.at[p - 1], span(1 - group), 1)

    if sections == 1:
        start_section(*weights[0])
    else:
        for s in range(sections):
            pl.when(meta[SECOND] == s)(partial(start_section, *weights[s]))

    square = jnp.zeros((hidden.shape[1], 1), jnp.float32)
    for k in range(4):
        piece = pieces[k][...] if count > 1 else pieces[0][:, k * width : (k + 1) * width]
        hidden[meta[HELD + k] if count > 1 else k] = piece
        wide = piece.astype(jnp.float32)
        square = square + jnp.sum(wide * wide, axis=1, keepdims=True)
    scale = lax.rsqrt(square / (4 * width) + 1e-05)

    for p in (1, 2, 0):
        for r in range(4):
            for q in range(2):
                pltpu.make_async_copy(
                    own_in.at[0, 0, pl.ds(0, part)], held.at[p, r, pl.ds(0, part)], held_sem.at[p, r, q]
                ).wait()
            product = jnp.dot(
                hidden[meta[rows[r]]], held[p, r], preferred_element_type=jnp.float32
            )
            if r == 0:
                total[p] = product
            else:
                total[p] += product
    query_ref[...] = (total[0] * scale).astype(query_ref.dtype)
    mixed_ref[...] = ((total[1] * scale) * (total[2] * scale)).astype(mixed_ref.dtype)


def project_in(meta, section, pieces, own_in, core_in, weights):
    width, channels = own_in.shape[2:]
    tokens = pieces[0].shape[0]
    sections = len(weights)
    far = pl.BlockSpec(memory_space=pl.ANY)
    vmem = pl.BlockSpec(memory_space=pltpu.VMEM)
    smem = pl.BlockSpec(memory_space=pltpu.SMEM)
    out = jax.ShapeDtypeStruct((tokens, channels), jnp.bfloat16)
    return pl.pallas_call(
        partial(in_kernel, sections),
        out_shape=(out, out),
        in_specs=[smem] * 2 + [vmem] * len(pieces) + [far] * (2 + sum(len(w) for w in weights)),
        out_specs=(vmem, vmem),
        scratch_shapes=[
            pltpu.VMEM((4, tokens, width), jnp.bfloat16),
            pltpu.VMEM((3, 4, width, channels), jnp.bfloat16),
            pltpu.VMEM((3, tokens, channels), jnp.float32),
            pltpu.SemaphoreType.DMA((3, 4, 2)),
        ],
        compiler_params=pltpu.CompilerParams(vmem_limit_bytes=24 * MIB),
        cost_estimate=pl.CostEstimate(
            flops=24 * tokens * width * channels,
            bytes_accessed=24 * width * channels,
            transcendentals=0,
        ),
        name="project_in",
    )(meta, section, *pieces, own_in, core_in, *[w for ws in weights for w in ws])


BLOCK = 64


def filter_kernel(meta, halo, mixed, query, bands, short, gated, extended):
    reach, tokens = halo.shape[0], mixed.shape[0]
    channels = mixed.shape[1]
    group_size = channels // (bands.shape[0] // BLOCK)

    @pl.when(meta[0] == 0)
    def _():
        extended[:reach] = halo[...].astype(jnp.float32)
        extended[reach:] = mixed[...].astype(jnp.float32)
        taps = short[...].astype(jnp.float32)
        total = jnp.zeros((tokens, channels), jnp.float32)
        for t in range(taps.shape[0]):
            total = total + taps[t : t + 1] * extended[reach - t : reach - t + tokens]
        gated[...] = (query[...].astype(jnp.float32) * total).astype(gated.dtype)

    @pl.when(meta[0] != 0)
    def _():
        lanes = 128
        per_tile = lanes // group_size
        lane_group = lax.broadcasted_iota(jnp.int32, (BLOCK, lanes), 1) // group_size
        for tile in range(channels // lanes):
            at = slice(tile * lanes, (tile + 1) * lanes)
            column = jnp.concatenate([halo[:, at], mixed[:, at]], 0)
            band = bands[tile * per_tile * BLOCK : (tile + 1) * per_tile * BLOCK]
            for b in range(tokens // BLOCK):
                window = column[b * BLOCK : b * BLOCK + reach + BLOCK]
                product = jnp.dot(band, window, preferred_element_type=jnp.float32)
                total = product[:BLOCK]
                for m in range(1, per_tile):
                    total = jnp.where(
                        lane_group == m, product[m * BLOCK : (m + 1) * BLOCK], total
                    )
                rows = slice(b * BLOCK, (b + 1) * BLOCK)
                gated[rows, at] = (query[rows, at].astype(jnp.float32) * total).astype(gated.dtype)


def filter_and_gate(section, halo, mixed, query, bands, short):
    tokens, channels = mixed.shape
    vmem = pl.BlockSpec(memory_space=pltpu.VMEM)
    return pl.pallas_call(
        filter_kernel,
        out_shape=jax.ShapeDtypeStruct(mixed.shape, jnp.bfloat16),
        in_specs=[pl.BlockSpec(memory_space=pltpu.SMEM)] + [vmem] * 5,
        out_specs=vmem,
        scratch_shapes=[pltpu.VMEM((halo.shape[0] + tokens, channels), jnp.float32)],
        compiler_params=pltpu.CompilerParams(vmem_limit_bytes=8 * MIB),
        cost_estimate=pl.CostEstimate(
            flops=2 * tokens * channels * 1024, bytes_accessed=8 * tokens * channels, transcendentals=0
        ),
        name="filter_and_gate",
    )(section, halo, mixed, query, bands, short)


def tap_bands(medium_taps):
    reach, groups = medium_taps.shape
    length = 2 * reach
    zero = jnp.zeros((groups, 1), medium_taps.dtype)
    tail = jnp.zeros((groups, reach - 1), medium_taps.dtype)
    cycle = jnp.concatenate([zero, medium_taps[::-1].T, tail], 1)
    skewed = jnp.broadcast_to(cycle[:, None], (groups, BLOCK, length)).reshape(groups, -1)
    skewed = skewed[:, : BLOCK * (length - 1)].reshape(groups, BLOCK, length - 1)
    return skewed[:, :, : reach + BLOCK].reshape(groups * BLOCK, reach + BLOCK)


def out_kernel(sections, meta, section_ref, *refs):
    own_gated, core_gated, own_hidden, core_hidden, near = refs[:5]
    weights = [refs[5 + 4 * s : 9 + 4 * s] for s in range(sections)]
    own_out, core_out, held, held_sem = refs[5 + 4 * sections :]
    tokens, width = own_hidden.shape
    part = width // 2
    group = meta[GROUP]
    section = section_ref[0]
    mine = pl.ds(pl.multiple_of(group * part, part), part)
    other = pl.ds(pl.multiple_of((1 - group) * part, part), part)

    def start(k, first, second):
        pltpu.make_async_copy(first, held.at[k, mine], held_sem.at[k, 0]).start()
        pltpu.make_async_copy(second, held.at[k, other], held_sem.at[k, 1]).start()

    def start_same(came, came_y, sent, sent_y):
        start(0, near.at[section, mine], near.at[section, other])
        for k in range(1, 4):
            start(k, came.at[k - 1], came_y.at[k - 1])

    def start_cross(came, came_y, sent, sent_y):
        for k in range(4):
            start(k, sent.at[k], sent_y.at[k])

    for s in range(sections):
        for same in range(2):
            here = meta[SAME] == same
            if sections > 1:
                here = jnp.logical_and(here, meta[SECOND] == s)
            pl.when(here)(partial(start_same if same else start_cross, *weights[s]))

    total = None
    for k in range(4):
        for n, at in enumerate((mine, other)):
            pltpu.make_async_copy(weights[0][0].at[0], held.at[k, at], held_sem.at[k, n]).wait()
        both = jnp.concatenate([own_gated[k], core_gated[k]], 0)
        product = lax.dot_general(
            both, held[k], (((1,), (1,)), ((), ())), preferred_element_type=jnp.float32
        )
        total = product if total is None else total + product
    own_out[...] = (own_hidden[...].astype(jnp.float32) + total[:tokens]).astype(own_out.dtype)
    core_out[...] = (core_hidden[...].astype(jnp.float32) + total[tokens:]).astype(core_out.dtype)


def project_out(meta, section, own_gated, core_gated, own_hidden, core_hidden, near, weights):
    tokens, width = own_hidden.shape
    channels = own_gated.shape[2]
    sections = len(weights)
    far = pl.BlockSpec(memory_space=pl.ANY)
    vmem = pl.BlockSpec(memory_space=pltpu.VMEM)
    smem = pl.BlockSpec(memory_space=pltpu.SMEM)
    out = jax.ShapeDtypeStruct((tokens, width), jnp.bfloat16)
    return pl.pallas_call(
        partial(out_kernel, sections),
        out_shape=(out, out),
        in_specs=[smem] * 2 + [vmem] * 4 + [far] * (1 + 4 * sections),
        out_specs=(vmem, vmem),
        scratch_shapes=[
            pltpu.VMEM((4, width, channels), jnp.bfloat16),
            pltpu.SemaphoreType.DMA((4, 2)),
        ],
        compiler_params=pltpu.CompilerParams(vmem_limit_bytes=16 * MIB),
        cost_estimate=pl.CostEstimate(
            flops=16 * tokens * width * channels,
            bytes_accessed=8 * width * channels,
            transcendentals=0,
        ),
        name="project_out",
    )(
        meta,
        section,
        own_gated,
        core_gated,
        own_hidden,
        core_hidden,
        near,
        *[w for ws in weights for w in ws],
    )


def taken_kernel(at, in_ref, out_ref, out_half, kv_half, query, sem):
    section = at[0]
    part = out_half.shape[0]
    mine = pl.ds(pl.multiple_of(at[1] * part, part), part)
    copies = [
        pltpu.make_async_copy(in_ref.at[section, 1, mine], kv_half.at[0], sem.at[0]),
        pltpu.make_async_copy(in_ref.at[section, 2, mine], kv_half.at[1], sem.at[1]),
        pltpu.make_async_copy(out_ref.at[section, mine], out_half, sem.at[2]),
        pltpu.make_async_copy(in_ref.at[section, 0], query, sem.at[3]),
    ]
    for copy in copies:
        copy.start()
    for copy in copies:
        copy.wait()


def taken(section, g, in_weights, out_weights):
    width, channels = out_weights.shape[1:]
    part = width // 2
    far = pl.BlockSpec(memory_space=pl.ANY)
    near = pl.BlockSpec(memory_space=pltpu.VMEM)
    shapes = [(part, channels), (2, part, channels), (width, channels)]
    return pl.pallas_call(
        taken_kernel,
        out_shape=tuple(jax.ShapeDtypeStruct(shape, jnp.bfloat16) for shape in shapes),
        in_specs=[pl.BlockSpec(memory_space=pltpu.SMEM), far, far],
        out_specs=(near,) * len(shapes),
        scratch_shapes=[pltpu.SemaphoreType.DMA((4,))],
        compiler_params=pltpu.CompilerParams(vmem_limit_bytes=8 * MIB),
        name="taken",
    )(jnp.stack([section, g]).astype(jnp.int32), in_weights, out_weights)


def after(value, *others):
    return lax.optimization_barrier((value,) + others)[0]


EVERY = ("groups", "ctx", "chan")
PLANE = ("ctx", "chan")


class Rounds:
    def __init__(self):
        self.before, self.now = [], []

    def __call__(self, value, axes, pairs):
        return self.join(after(value, *self.before) if self.before else value, axes, pairs)

    def join(self, value, axes, pairs):
        self.now.append(lax.ppermute(value, axes, pairs))
        return self.now[-1]

    def turn(self):
        self.before, self.now = self.now, []


def along(k):
    return [
        (flat(2 * x + (j % 2), (j - k) % 4), flat(3 * x, j)) for x in range(2) for j in range(4)
    ]


def over_chips(source):
    return [(flat(source(x, j), j), flat(2 - x, j)) for x in range(2) for j in range(4)]


def over_groups(core):
    return [
        (flat(core(x), j, q), flat(core(x), j, 1 - q))
        for x in range(2)
        for j in range(4)
        for q in range(2)
    ]


CORES = ctx_pairs(1)
CHIPS = ctx_pairs(2)
GROUPS = [(0, 1), (1, 0)]
FROM_HOLDER = over_chips(lambda x, j: 2 * x + j % 2)
FROM_SAME = over_chips(lambda x, j: 3 * x)
SWAP_SAME = over_groups(lambda x: 3 * x)
SWAP_CROSS = over_groups(lambda x: 2 - x)
BESIDE = [(s, s ^ 1) for s in range(4)]
HALO = [(0, 1), (1, 2), (2, 3)]


def around(k):
    return [(s, (s + k) % 4) for s in range(4)]


def shards(stream, in_weights, out_weights, short_taps, medium_taps, plan):
    g, i, j = lax.axis_index("groups"), lax.axis_index("ctx"), lax.axis_index("chan")
    x, c, h = i // 2, i % 2, j % 2
    first = plan[0]
    reach = medium_taps.shape[0]
    width = stream.shape[1]
    part = width // 2
    in_weights = in_weights.transpose(0, 2, 1, 3)
    near = (j // 2) == c
    send = Rounds()
    bands = tap_bands(medium_taps)

    whole = lax.all_gather(stream, "chan", axis=1, tiled=True)
    send.now.append(whole)
    out_a, kv_a, q_a = taken(first, g, in_weights, out_weights)
    x_kv = send(kv_a, "ctx", CHIPS)
    x_q = send(q_a, "ctx", CHIPS)
    core_in = send(after(in_weights, q_a), "ctx", CORES)
    near_out = send(after(out_weights, q_a), PLANE, along(0))
    out_b, kv_b, q_b = taken(after(1 - first, q_a), g, in_weights, out_weights)
    send.now += [out_b, bands]

    def near_half(section):
        return lax.dynamic_slice(near_out, (section, g * part, 0), (1, part, near_out.shape[2]))

    send.turn()
    c_kv = send(x_kv, "ctx", CORES)
    c_q = send(x_q, "ctx", CORES)
    y_kv = send(x_kv, "groups", GROUPS)
    x_kv_b = send(kv_b, "ctx", CHIPS)
    z_a = {k: send(out_a, PLANE, along(k)) for k in (2, 1, 3)}

    send.turn()
    cy_kv = send(y_kv, "ctx", CORES)
    rest_a = jnp.stack([z_a[1], z_a[2], z_a[3]])
    sent_a = send(jnp.concatenate([near_half(first), rest_a]), PLANE, FROM_SAME)
    rest_y = send(rest_a, EVERY, SWAP_SAME)
    z_b = {k: send(out_b, PLANE, along(k)) for k in (2, 1, 3)}
    rest_b = jnp.stack([z_b[1], z_b[2], z_b[3]])

    send.turn()
    sent_y = send(sent_a, EVERY, SWAP_CROSS)
    x_q_b = send(q_b, "ctx", CHIPS)
    weights_in = [[x_kv, y_kv, c_kv, cy_kv, x_q, c_q]]
    weights_out = [[rest_a, rest_y, sent_a, sent_y]]

    own_hidden = lax.dynamic_slice_in_dim(whole, (2 * c + h) * width, width, 1)
    to_core = lax.dynamic_slice_in_dim(whole, (2 * (1 - c) + h) * width, width, 1)
    core_hidden = lax.ppermute(to_core, "ctx", CORES)
    pieces, slices = [whole], []

    for step in range(STEPS):
        count = 1 if step == 0 else 2
        section = plan[step]
        second = (section != first).astype(jnp.int32)
        section = section.reshape(1)
        scalars = [second, g, (x == c).astype(jnp.int32), i, i ^ 1, i ^ 2, i ^ 3] + slices
        meta = jnp.stack([jnp.asarray(s, jnp.int32) for s in scalars])
        query, mixed = project_in(meta, section, pieces, in_weights, core_in, weights_in[:count])
        halo = lax.ppermute(mixed[-reach:], "ctx", HALO)
        gated = filter_and_gate(section, halo, mixed, query, bands, short_taps)
        g_2, g_3, g_1 = (send.join(gated, "chan", around(k)) for k in (2, 3, 1))
        if step == 0:
            send.turn()
            y_kv_b = send(x_kv_b, "groups", GROUPS)
            sent_b = send(jnp.concatenate([near_half(1 - first), rest_b]), PLANE, FROM_SAME)
        own_gated = jnp.stack([gated, g_1, g_2, g_3])
        core_gated = lax.ppermute(own_gated, "ctx", CORES)
        own_hidden, core_hidden = project_out(
            meta,
            section,
            own_gated,
            core_gated,
            own_hidden,
            core_hidden,
            near_out,
            weights_out[:count],
        )
        swapped = lax.ppermute(core_hidden, "ctx", CORES)
        if step == STEPS - 1:
            return jnp.where(near, own_hidden, swapped)
        beside = send.join(own_hidden, "chan", BESIDE)
        beside_core = send.join(swapped, "chan", BESIDE)
        pieces = [own_hidden, swapped, beside, beside_core]
        slices = [2 * c + h, 2 * (1 - c) + h, 2 * c + 1 - h, 2 * (1 - c) + 1 - h]
        if step == 0:
            send.turn()
            c_q_b = send(x_q_b, "ctx", CORES)
            cy_kv_b = send(y_kv_b, "ctx", CORES)
            c_kv_b = send(x_kv_b, "ctx", CORES)
            rest_b_y = send(rest_b, EVERY, SWAP_SAME)
            sent_b_y = send(sent_b, EVERY, SWAP_CROSS)
            weights_in.append([x_kv_b, y_kv_b, c_kv_b, cy_kv_b, x_q_b, c_q_b])
            weights_out.append([rest_b, rest_b_y, sent_b, sent_b_y])


def solution(mesh):
    special = dict(mesh.shape) == {"groups": 2, "ctx": 4, "chan": 4}
    return jax.shard_map(
        shards if special else general_shards,
        mesh=mesh,
        in_specs=(
            P(("groups", "ctx"), "chan"),
            P(None, "ctx", None, "chan"),
            P(None, "ctx", "chan"),
            P(None, "chan"),
            P(None, "chan"),
            P(),
        ),
        out_specs=P(("groups", "ctx"), "chan"),
        check_vma=False,
    )
```

```python
from functools import partial

import jax
import jax.numpy as jnp
from jax import lax
from jax.experimental import pallas as pl
from jax.experimental.pallas import tpu as pltpu
from jax.sharding import PartitionSpec as P

STEPS = 4
MIB = 1024 * 1024


def passed_along(value, axis, steps):
    count = lax.axis_size(axis)
    leading, last = (max(0, -steps), min(count, count - steps))
    return lax.ppermute(value, axis, [(source, source + steps) for source in range(leading, last)])


def section_taps(section, short_taps, medium_taps):
    reach = medium_taps.shape[0]
    channels = short_taps.shape[1]
    padding = jnp.zeros((reach - short_taps.shape[0], channels), short_taps.dtype)
    short_full = jnp.concatenate([short_taps, padding], 0)
    group_size = channels // medium_taps.shape[1]
    medium_full = jnp.broadcast_to(
        medium_taps[:, :, None], (reach, medium_taps.shape[1], group_size)
    ).reshape(reach, channels)
    return jnp.where(section == 0, short_full, medium_full)


def causal_filter(extended, filter_taps):
    filtered = lax.conv_general_dilated(
        extended[None],
        filter_taps[::-1][:, None, :],
        (1,),
        "VALID",
        dimension_numbers=("NWC", "WIO", "NWC"),
        feature_group_count=filter_taps.shape[1],
        preferred_element_type=jnp.float32,
    )
    return filtered[0]


def filter_gate(projected, section, short_taps, medium_taps):
    query_bf = projected[:, 0].astype(jnp.bfloat16)
    mixed_bf = (projected[:, 1] * projected[:, 2]).astype(jnp.bfloat16)
    reach = medium_taps.shape[0]
    earlier = passed_along(mixed_bf[-reach:], "ctx", 1)
    extended = jnp.concatenate([earlier[1:], mixed_bf], 0)
    filtered = causal_filter(extended, section_taps(section, short_taps, medium_taps))
    return (query_bf.astype(jnp.float32) * filtered).astype(jnp.bfloat16)


def general_shards(stream, in_weights, out_weights, short_taps, medium_taps, plan):
    hidden = stream
    weights_in = lax.all_gather(in_weights, "ctx", axis=1, tiled=True)
    weights_out = lax.all_gather(out_weights, "ctx", axis=1, tiled=True)
    for step in range(STEPS):
        section = plan[step]
        full_rows = lax.all_gather(hidden, "chan", axis=1, tiled=True)
        widened = full_rows.astype(jnp.float32)
        row_scale = lax.rsqrt(jnp.mean(widened * widened, axis=1, keepdims=True) + 1e-05)
        chosen = lax.dynamic_index_in_dim(weights_in, section, 0, keepdims=False)
        projected = jnp.dot(
            full_rows, chosen.reshape(chosen.shape[0], -1), preferred_element_type=jnp.float32
        )
        projected = projected.reshape(full_rows.shape[0], 3, -1) * row_scale[:, :, None]
        gated = filter_gate(projected, section, short_taps, medium_taps)
        chosen = lax.dynamic_index_in_dim(weights_out, section, 0, keepdims=False)
        product = lax.dot_general(
            gated, chosen, (((1,), (1,)), ((), ())), preferred_element_type=jnp.float32
        )
        update = lax.psum_scatter(
            product.astype(jnp.bfloat16), "chan", scatter_dimension=1, tiled=True
        ).astype(jnp.float32)
        hidden = (hidden.astype(jnp.float32) + update).astype(jnp.bfloat16)
    return hidden


SECOND, GROUP, SAME, MATCH, ROW = range(5)


def ctx_pairs(change):
    return [(i, i ^ change) for i in range(4)]


def flat(i, j, g=None):
    return (i * 4 + j) if g is None else (g * 16 + i * 4 + j)


OWN, CORE, CHIP, BOTH = range(4)


def in_kernel(mode, sections, meta, section_ref, *refs):
    count = 1 if mode == "whole" else 2
    pieces, refs = refs[:count], refs[count:]
    if mode == "last":
        earlier, earlier_square, refs = refs[0], refs[1], refs[2:]
    own_in, core_in = refs[:2]
    weights = [refs[2 + 5 * s : 7 + 5 * s] for s in range(sections)]
    out_ref, out_ref2, hidden, held, total, held_sem = refs[2 + 5 * sections :]
    tokens, width = hidden.shape[1:]
    part = width // 2
    group = meta[GROUP]
    section = section_ref[0]
    slots = held.shape[1]

    def span(q):
        return pl.ds(pl.multiple_of(q * part, part), part)

    def start(kind, p, slot, sources):
        chip, chip_y, chip_q, both = sources[:4]
        if kind in (OWN, CORE):
            source = own_in if kind == OWN else core_in
            halves = [(source.at[section, p, span(q)], span(q)) for q in range(2)]
        elif p == 0:
            sources = chip_q if kind == CHIP else both
            halves = [(sources.at[q], span(q)) for q in range(2)]
        elif kind == CHIP:
            halves = [(chip.at[p - 1], span(group)), (chip_y.at[p - 1], span(1 - group))]
        else:
            halves = [(sources[4].at[p - 1], span(group)), (both.at[p + 1], span(1 - group))]
        for q in range(2):
            pltpu.make_async_copy(
                halves[q][0], held.at[p, slot, halves[q][1]], held_sem.at[p, slot, q]
            ).start()

    def start_kinds(kinds, sources):
        for p in (1, 2, 0):
            for slot, kind in enumerate(kinds):
                start(kind, p, slot, sources)

    if mode == "whole":
        start_kinds((OWN, CORE, CHIP, BOTH), weights[0])
    else:
        for match in range(2):
            kinds = (OWN, CHIP) if match == (mode == "first") else (CORE, BOTH)
            for s in range(sections):
                here = jnp.logical_and(meta[MATCH] == match, meta[SECOND] == s)
                pl.when(here)(partial(start_kinds, kinds, weights[s]))

    square = jnp.zeros((tokens, 1), jnp.float32)
    for k in range(slots):
        if mode == "whole":
            piece = pieces[0][:, k * width : (k + 1) * width]
            hidden[k] = piece
        else:
            piece = pieces[k][...]
            hidden[1 - meta[SAME] if k == 0 else meta[SAME]] = piece
        wide = piece.astype(jnp.float32)
        square = square + jnp.sum(wide * wide, axis=1, keepdims=True)
    if mode == "last":
        square = square + earlier_square[:, :1]
    if mode == "first":
        out_ref2[...] = jnp.broadcast_to(square, out_ref2.shape)
    else:
        scale = lax.rsqrt(square / (4 * width) + 1e-05)

    for p in (1, 2, 0):
        for slot in range(slots):
            for q in range(2):
                pltpu.make_async_copy(
                    own_in.at[0, 0, pl.ds(0, part)],
                    held.at[p, slot, pl.ds(0, part)],
                    held_sem.at[p, slot, q],
                ).wait()
            at = meta[ROW + slot] if mode == "whole" else slot
            product = jnp.dot(hidden[at], held[p, slot], preferred_element_type=jnp.float32)
            if slot > 0:
                total[p] += product
            elif mode == "last":
                total[p] = earlier[p] + product
            else:
                total[p] = product
    if mode == "first":
        out_ref[...] = total[...]
    else:
        out_ref[...] = (total[0] * scale).astype(out_ref.dtype)
        out_ref2[...] = ((total[1] * scale) * (total[2] * scale)).astype(out_ref2.dtype)


def project_in(mode, meta, section, pieces, earlier, own_in, core_in, weights):
    width, channels = own_in.shape[2:]
    tokens = pieces[0].shape[0]
    sections = len(weights)
    slots = 4 if mode == "whole" else 2
    anywhere = pl.BlockSpec(memory_space=pl.ANY)
    vmem = pl.BlockSpec(memory_space=pltpu.VMEM)
    smem = pl.BlockSpec(memory_space=pltpu.SMEM)
    if mode == "first":
        out = (
            jax.ShapeDtypeStruct((3, tokens, channels), jnp.float32),
            jax.ShapeDtypeStruct((tokens, 128), jnp.float32),
        )
    else:
        out = (jax.ShapeDtypeStruct((tokens, channels), jnp.bfloat16),) * 2
    return pl.pallas_call(
        partial(in_kernel, mode, sections),
        out_shape=out,
        in_specs=[smem] * 2
        + [vmem] * (len(pieces) + len(earlier))
        + [anywhere] * (2 + sum(len(w) for w in weights)),
        out_specs=(vmem, vmem),
        scratch_shapes=[
            pltpu.VMEM((slots, tokens, width), jnp.bfloat16),
            pltpu.VMEM((3, slots, width, channels), jnp.bfloat16),
            pltpu.VMEM((3, tokens, channels), jnp.float32),
            pltpu.SemaphoreType.DMA((3, slots, 2)),
        ],
        compiler_params=pltpu.CompilerParams(vmem_limit_bytes=44 * MIB),
        cost_estimate=pl.CostEstimate(
            flops=6 * slots * tokens * width * channels,
            bytes_accessed=6 * slots * width * channels,
            transcendentals=0,
        ),
        name="project_in_" + mode,
    )(meta, section, *pieces, *earlier, own_in, core_in, *[w for ws in weights for w in ws])


BLOCK = 64


def filter_kernel(meta, halo, mixed, query, bands, short, gated, extended):
    reach, tokens = halo.shape[0], mixed.shape[0]
    channels = mixed.shape[1]
    group_size = channels // (bands.shape[0] // BLOCK)

    @pl.when(meta[0] == 0)
    def _():
        extended[:reach] = halo[...].astype(jnp.float32)
        extended[reach:] = mixed[...].astype(jnp.float32)
        taps = short[...].astype(jnp.float32)
        total = jnp.zeros((tokens, channels), jnp.float32)
        for t in range(taps.shape[0]):
            total = total + taps[t : t + 1] * extended[reach - t : reach - t + tokens]
        gated[...] = (query[...].astype(jnp.float32) * total).astype(gated.dtype)

    @pl.when(meta[0] != 0)
    def _():
        lanes = 128
        per_tile = lanes // group_size
        lane_group = lax.broadcasted_iota(jnp.int32, (BLOCK, lanes), 1) // group_size
        for tile in range(channels // lanes):
            at = slice(tile * lanes, (tile + 1) * lanes)
            column = jnp.concatenate([halo[:, at], mixed[:, at]], 0)
            band = bands[tile * per_tile * BLOCK : (tile + 1) * per_tile * BLOCK]
            for b in range(tokens // BLOCK):
                window = column[b * BLOCK : b * BLOCK + reach + BLOCK]
                product = jnp.dot(band, window, preferred_element_type=jnp.float32)
                total = product[:BLOCK]
                for m in range(1, per_tile):
                    total = jnp.where(
                        lane_group == m, product[m * BLOCK : (m + 1) * BLOCK], total
                    )
                rows = slice(b * BLOCK, (b + 1) * BLOCK)
                gated[rows, at] = (query[rows, at].astype(jnp.float32) * total).astype(gated.dtype)


def filter_and_gate(section, halo, mixed, query, bands, short):
    tokens, channels = mixed.shape
    vmem = pl.BlockSpec(memory_space=pltpu.VMEM)
    return pl.pallas_call(
        filter_kernel,
        out_shape=jax.ShapeDtypeStruct(mixed.shape, jnp.bfloat16),
        in_specs=[pl.BlockSpec(memory_space=pltpu.SMEM)] + [vmem] * 5,
        out_specs=vmem,
        scratch_shapes=[pltpu.VMEM((halo.shape[0] + tokens, channels), jnp.float32)],
        compiler_params=pltpu.CompilerParams(vmem_limit_bytes=8 * MIB),
        cost_estimate=pl.CostEstimate(
            flops=2 * tokens * channels * 1024, bytes_accessed=8 * tokens * channels, transcendentals=0
        ),
        name="filter_and_gate",
    )(section, halo, mixed, query, bands, short)


def tap_bands(medium_taps):
    reach, groups = medium_taps.shape
    length = 2 * reach
    zero = jnp.zeros((groups, 1), medium_taps.dtype)
    tail = jnp.zeros((groups, reach - 1), medium_taps.dtype)
    cycle = jnp.concatenate([zero, medium_taps[::-1].T, tail], 1)
    skewed = jnp.broadcast_to(cycle[:, None], (groups, BLOCK, length)).reshape(groups, -1)
    skewed = skewed[:, : BLOCK * (length - 1)].reshape(groups, BLOCK, length - 1)
    return skewed[:, :, : reach + BLOCK].reshape(groups * BLOCK, reach + BLOCK)


def out_kernel(sections, meta, *refs):
    own_gated, core_gated, own_hidden, core_hidden = refs[:4]
    weights = [refs[4 + 5 * s : 9 + 5 * s] for s in range(sections)]
    own_out, core_out, held, held_sem = refs[4 + 5 * sections :]
    tokens, width = own_hidden.shape
    part = width // 2
    group = meta[GROUP]
    mine = pl.ds(pl.multiple_of(group * part, part), part)
    other = pl.ds(pl.multiple_of((1 - group) * part, part), part)

    def start(first, second):
        for k in range(4):
            pltpu.make_async_copy(first.at[k], held.at[k, mine], held_sem.at[k, 0]).start()
            pltpu.make_async_copy(second.at[k], held.at[k, other], held_sem.at[k, 1]).start()

    for s in range(sections):
        shard, same_mine, same_other, cross_mine, cross_other = weights[s]
        cases = (
            (meta[SAME] == 0, cross_mine, cross_other),
            (meta[SAME] + meta[MATCH] == 2, shard, same_other),
            (meta[SAME] - meta[MATCH] == 1, same_mine, same_other),
        )
        for here, first, second in cases:
            if sections > 1:
                here = jnp.logical_and(here, meta[SECOND] == s)
            pl.when(here)(partial(start, first, second))

    total = None
    for k in range(4):
        for n, at in enumerate((mine, other)):
            pltpu.make_async_copy(weights[0][0].at[0], held.at[k, at], held_sem.at[k, n]).wait()
        both = jnp.concatenate([own_gated[k], core_gated[k]], 0)
        product = lax.dot_general(
            both, held[k], (((1,), (1,)), ((), ())), preferred_element_type=jnp.float32
        )
        total = product if total is None else total + product
    own_out[...] = (own_hidden[...].astype(jnp.float32) + total[:tokens]).astype(own_out.dtype)
    core_out[...] = (core_hidden[...].astype(jnp.float32) + total[tokens:]).astype(core_out.dtype)


def project_out(meta, own_gated, core_gated, own_hidden, core_hidden, weights):
    tokens, width = own_hidden.shape
    channels = own_gated.shape[2]
    sections = len(weights)
    anywhere = pl.BlockSpec(memory_space=pl.ANY)
    vmem = pl.BlockSpec(memory_space=pltpu.VMEM)
    smem = pl.BlockSpec(memory_space=pltpu.SMEM)
    out = jax.ShapeDtypeStruct((tokens, width), jnp.bfloat16)
    return pl.pallas_call(
        partial(out_kernel, sections),
        out_shape=(out, out),
        in_specs=[smem] + [vmem] * 4 + [anywhere] * (5 * sections),
        out_specs=(vmem, vmem),
        scratch_shapes=[
            pltpu.VMEM((4, width, channels), jnp.bfloat16),
            pltpu.SemaphoreType.DMA((4, 2)),
        ],
        compiler_params=pltpu.CompilerParams(vmem_limit_bytes=16 * MIB),
        cost_estimate=pl.CostEstimate(
            flops=16 * tokens * width * channels,
            bytes_accessed=8 * width * channels,
            transcendentals=0,
        ),
        name="project_out",
    )(meta, own_gated, core_gated, own_hidden, core_hidden, *[w for ws in weights for w in ws])


def taken_kernel(at, in_ref, out_ref, out_half, kv_half, query, sem):
    section = at[0]
    part = out_half.shape[0]
    mine = pl.ds(pl.multiple_of(at[1] * part, part), part)
    copies = [
        pltpu.make_async_copy(in_ref.at[section, 1, mine], kv_half.at[0], sem.at[0]),
        pltpu.make_async_copy(in_ref.at[section, 2, mine], kv_half.at[1], sem.at[1]),
        pltpu.make_async_copy(out_ref.at[section, mine], out_half, sem.at[2]),
        pltpu.make_async_copy(in_ref.at[section, 0, pl.ds(0, part)], query.at[0], sem.at[3]),
        pltpu.make_async_copy(in_ref.at[section, 0, pl.ds(part, part)], query.at[1], sem.at[4]),
    ]
    for copy in copies:
        copy.start()
    for copy in copies:
        copy.wait()


def taken(section, g, in_weights, out_weights):
    width, channels = out_weights.shape[1:]
    part = width // 2
    far = pl.BlockSpec(memory_space=pl.ANY)
    near = pl.BlockSpec(memory_space=pltpu.VMEM)
    shapes = [(part, channels), (2, part, channels), (2, part, channels)]
    return pl.pallas_call(
        taken_kernel,
        out_shape=tuple(jax.ShapeDtypeStruct(shape, jnp.bfloat16) for shape in shapes),
        in_specs=[pl.BlockSpec(memory_space=pltpu.SMEM), far, far],
        out_specs=(near,) * len(shapes),
        scratch_shapes=[pltpu.SemaphoreType.DMA((5,))],
        compiler_params=pltpu.CompilerParams(vmem_limit_bytes=8 * MIB),
        name="taken",
    )(jnp.stack([section, g]).astype(jnp.int32), in_weights, out_weights)


def after(value, *others):
    return lax.optimization_barrier((value,) + others)[0]


EVERY = ("groups", "ctx", "chan")
PLANE = ("ctx", "chan")


class Rounds:
    def __init__(self):
        self.before, self.now = [], []

    def __call__(self, value, axes, pairs):
        return self.join(after(value, *self.before) if self.before else value, axes, pairs)

    def join(self, value, axes, pairs):
        self.now.append(lax.ppermute(value, axes, pairs))
        return self.now[-1]

    def turn(self):
        self.before, self.now = self.now, []


def holder(x, j):
    return 2 * x + j % 2


def keeper(x, j):
    return 3 * x


def other_keeper(x, j):
    return 2 - x


def plane_pairs(source, target):
    return [(flat(source(x, j), j), flat(target(x, j), j)) for x in range(2) for j in range(4)]


def group_pairs(source, target):
    return [
        (flat(source(x, j), j, q), flat(target(x, j), j, 1 - q))
        for x in range(2)
        for j in range(4)
        for q in range(2)
    ]


CORES = ctx_pairs(1)
CHIPS = ctx_pairs(2)
GROUPS = [(0, 1), (1, 0)]
ALONG = {
    k: [(flat(holder(x, j), (j - k) % 4), flat(holder(x, j), j)) for x in range(2) for j in range(4)]
    for k in (1, 2, 3)
}
TO_KEEPER = [pair for pair in plane_pairs(holder, keeper) if pair[0] != pair[1]]
TO_OTHER_KEEPER = plane_pairs(holder, other_keeper)
TO_KEEPER_OVER = group_pairs(holder, keeper)
OTHER_KEEPERS_OVER = group_pairs(other_keeper, other_keeper)
BESIDE = [(s, s ^ 1) for s in range(4)]
HALO = [(0, 1), (1, 2), (2, 3)]


def around(k):
    return [(s, (s + k) % 4) for s in range(4)]


def shards(stream, in_weights, out_weights, short_taps, medium_taps, plan):
    g, i, j = lax.axis_index("groups"), lax.axis_index("ctx"), lax.axis_index("chan")
    x, c, h = i // 2, i % 2, j % 2
    first = plan[0]
    reach = medium_taps.shape[0]
    width = stream.shape[1]
    part = width // 2
    in_weights = in_weights.transpose(0, 2, 1, 3)
    near = (j // 2) == c
    send = Rounds()
    bands = tap_bands(medium_taps)

    whole = lax.all_gather(stream, "chan", axis=1, tiled=True)
    send.now.append(whole)
    out_a, kv_a, q_a = taken(first, g, in_weights, out_weights)
    x_kv = send(kv_a, "ctx", CHIPS)
    x_q = send(q_a, "ctx", CHIPS)
    core_in = send(after(in_weights, q_a), "ctx", CORES)
    out_b, kv_b, q_b = taken(after(1 - first, q_a), g, in_weights, out_weights)
    send.now += [out_b, bands]

    send.turn()
    y_kv = send(x_kv, "groups", GROUPS)
    c_kv = lax.ppermute(x_kv, "ctx", CORES)
    x_kv_b = send(kv_b, "ctx", CHIPS)
    shard_a = [out_a] + [send(out_a, PLANE, ALONG[k]) for k in (1, 2, 3)]

    send.turn()
    shard_a = jnp.stack(shard_a)
    cross_a = send(shard_a, PLANE, TO_OTHER_KEEPER)
    same_y = send(shard_a, EVERY, TO_KEEPER_OVER)
    both = send(jnp.concatenate([x_q, y_kv]), "ctx", CORES)
    same_a = send(shard_a, PLANE, TO_KEEPER)
    shard_b = [out_b] + [send(after(out_b, both, same_a), PLANE, ALONG[k]) for k in (1, 2, 3)]

    send.turn()
    shard_b = jnp.stack(shard_b)
    cross_y = send(cross_a, EVERY, OTHER_KEEPERS_OVER)
    weights_in = [[x_kv, y_kv, x_q, both, c_kv]]
    weights_out = [[shard_a, same_a, same_y, cross_a, cross_y]]

    own_hidden = lax.dynamic_slice_in_dim(whole, (2 * c + h) * width, width, 1)
    to_core = lax.dynamic_slice_in_dim(whole, (2 * (1 - c) + h) * width, width, 1)
    core_hidden = lax.ppermute(to_core, "ctx", CORES)
    inputs = in_weights, core_in

    for step in range(STEPS):
        count = 1 if step == 0 else 2
        section = plan[step]
        second = (section != first).astype(jnp.int32)
        section = section.reshape(1)
        scalars = [second, g, (x == c).astype(jnp.int32), (c == h).astype(jnp.int32)]
        scalars += [i, i ^ 1, i ^ 2, i ^ 3]
        meta = jnp.stack([jnp.asarray(s, jnp.int32) for s in scalars])
        if step == 0:
            query, mixed = project_in("whole", meta, section, [whole], [], *inputs, weights_in)
        else:
            part_sums = project_in("first", meta, section, near_pieces, [], *inputs, weights_in)
            query, mixed = project_in("last", meta, section, far_pieces, part_sums, *inputs, weights_in)
        halo = lax.ppermute(mixed[-reach:], "ctx", HALO)
        if step == 0:
            c_kv_b = lax.ppermute(after(x_kv_b, halo), "ctx", CORES)
        gated = filter_and_gate(section, halo, mixed, query, bands, short_taps)
        if step == 0:
            cross_b = send(after(shard_b, halo), PLANE, TO_OTHER_KEEPER)
        g_2, g_3, g_1 = (send.join(gated, "chan", around(k)) for k in (2, 3, 1))
        if step == 0:
            send.turn()
            y_kv_b = send(x_kv_b, "groups", GROUPS)
            x_q_b = send(q_b, "ctx", CHIPS)
        own_gated = jnp.stack([gated, g_1, g_2, g_3])
        core_gated = lax.ppermute(own_gated, "ctx", CORES)
        own_hidden, core_hidden = project_out(
            meta, own_gated, core_gated, own_hidden, core_hidden, weights_out[:count]
        )
        swapped = lax.ppermute(core_hidden, "ctx", CORES)
        if step == STEPS - 1:
            return jnp.where((j // 2) == c, own_hidden, swapped)
        near_pieces = [own_hidden, swapped]
        far_pieces = [send.join(piece, "chan", BESIDE) for piece in near_pieces]
        if step == 0:
            send.turn()
            both_b = send(jnp.concatenate([x_q_b, y_kv_b]), "ctx", CORES)
            same_b_y = send(shard_b, EVERY, TO_KEEPER_OVER)
            same_b = send(shard_b, PLANE, TO_KEEPER)
            cross_b_y = send(cross_b, EVERY, OTHER_KEEPERS_OVER)
            weights_in.append([x_kv_b, y_kv_b, x_q_b, both_b, c_kv_b])
            weights_out.append([shard_b, same_b, same_b_y, cross_b, cross_b_y])


def solution(mesh):
    special = dict(mesh.shape) == {"groups": 2, "ctx": 4, "chan": 4}
    return jax.shard_map(
        shards if special else general_shards,
        mesh=mesh,
        in_specs=(
            P(("groups", "ctx"), "chan"),
            P(None, "ctx", None, "chan"),
            P(None, "ctx", "chan"),
            P(None, "chan"),
            P(None, "chan"),
            P(),
        ),
        out_specs=P(("groups", "ctx"), "chan"),
        check_vma=False,
    )
```

```python
from functools import partial

import jax
import jax.numpy as jnp
from jax import lax
from jax.experimental import pallas as pl
from jax.experimental.pallas import tpu as pltpu
from jax.sharding import PartitionSpec as P

STEPS = 4
MIB = 1024 * 1024


def passed_along(value, axis, steps):
    count = lax.axis_size(axis)
    leading, last = (max(0, -steps), min(count, count - steps))
    return lax.ppermute(value, axis, [(source, source + steps) for source in range(leading, last)])


def section_taps(section, short_taps, medium_taps):
    reach = medium_taps.shape[0]
    channels = short_taps.shape[1]
    padding = jnp.zeros((reach - short_taps.shape[0], channels), short_taps.dtype)
    short_full = jnp.concatenate([short_taps, padding], 0)
    group_size = channels // medium_taps.shape[1]
    medium_full = jnp.broadcast_to(
        medium_taps[:, :, None], (reach, medium_taps.shape[1], group_size)
    ).reshape(reach, channels)
    return jnp.where(section == 0, short_full, medium_full)


def causal_filter(extended, filter_taps):
    filtered = lax.conv_general_dilated(
        extended[None],
        filter_taps[::-1][:, None, :],
        (1,),
        "VALID",
        dimension_numbers=("NWC", "WIO", "NWC"),
        feature_group_count=filter_taps.shape[1],
        preferred_element_type=jnp.float32,
    )
    return filtered[0]


def filter_gate(projected, section, short_taps, medium_taps):
    query_bf = projected[:, 0].astype(jnp.bfloat16)
    mixed_bf = (projected[:, 1] * projected[:, 2]).astype(jnp.bfloat16)
    reach = medium_taps.shape[0]
    earlier = passed_along(mixed_bf[-reach:], "ctx", 1)
    extended = jnp.concatenate([earlier[1:], mixed_bf], 0)
    filtered = causal_filter(extended, section_taps(section, short_taps, medium_taps))
    return (query_bf.astype(jnp.float32) * filtered).astype(jnp.bfloat16)


def general_shards(stream, in_weights, out_weights, short_taps, medium_taps, plan):
    hidden = stream
    weights_in = lax.all_gather(in_weights, "ctx", axis=1, tiled=True)
    weights_out = lax.all_gather(out_weights, "ctx", axis=1, tiled=True)
    for step in range(STEPS):
        section = plan[step]
        full_rows = lax.all_gather(hidden, "chan", axis=1, tiled=True)
        widened = full_rows.astype(jnp.float32)
        row_scale = lax.rsqrt(jnp.mean(widened * widened, axis=1, keepdims=True) + 1e-05)
        chosen = lax.dynamic_index_in_dim(weights_in, section, 0, keepdims=False)
        projected = jnp.dot(
            full_rows, chosen.reshape(chosen.shape[0], -1), preferred_element_type=jnp.float32
        )
        projected = projected.reshape(full_rows.shape[0], 3, -1) * row_scale[:, :, None]
        gated = filter_gate(projected, section, short_taps, medium_taps)
        chosen = lax.dynamic_index_in_dim(weights_out, section, 0, keepdims=False)
        product = lax.dot_general(
            gated, chosen, (((1,), (1,)), ((), ())), preferred_element_type=jnp.float32
        )
        update = lax.psum_scatter(
            product.astype(jnp.bfloat16), "chan", scatter_dimension=1, tiled=True
        ).astype(jnp.float32)
        hidden = (hidden.astype(jnp.float32) + update).astype(jnp.bfloat16)
    return hidden


SECOND, GROUP, SAME, MATCH, ROW = range(5)


def scalars(plan, step):
    g, i, j = lax.axis_index("groups"), lax.axis_index("ctx"), lax.axis_index("chan")
    x, c, h = i >> 1, i & 1, j & 1
    second = (plan[step] != plan[0]).astype(jnp.int32)
    same, match = (x == c).astype(jnp.int32), (c == h).astype(jnp.int32)
    return [second, g, same, match, i, i ^ 1, i ^ 2, i ^ 3]


def ctx_pairs(change):
    return [(i, i ^ change) for i in range(4)]


def flat(i, j, g=None):
    return (i * 4 + j) if g is None else (g * 16 + i * 4 + j)


OWN, CORE, CHIP, BOTH = range(4)


def in_kernel(mode, step, sections, plan, *refs):
    meta = scalars(plan, step)
    section = plan[step]
    count = 1 if mode == "whole" else 2
    pieces, refs = refs[:count], refs[count:]
    if mode == "last":
        earlier, earlier_square, refs = refs[0], refs[1], refs[2:]
    own_in, core_in = refs[:2]
    weights, refs = [refs[2:6], refs[6:11]], refs[6 if sections == 1 else 11 :]
    out_ref, out_ref2, hidden, held, total, held_sem = refs
    tokens, width = hidden.shape[1:]
    part = width // 2
    group = meta[GROUP]
    slots = held.shape[1]

    def span(q):
        return pl.ds(pl.multiple_of(q * part, part), part)

    def start(kind, p, slot, sources):
        if kind in (OWN, CORE):
            source = own_in if kind == OWN else core_in
            halves = [(source.at[section, p, span(q)], span(q)) for q in range(2)]
        elif len(sources) == 4:
            mine, other = sources[:2] if kind == CHIP else sources[2:]
            halves = [(mine.at[p], span(group)), (other.at[p], span(1 - group))]
        elif p == 0:
            source = sources[2 if kind == CHIP else 3]
            halves = [(source.at[q], span(q)) for q in range(2)]
        else:
            mine, other, at = (sources[0], sources[1], p - 1) if kind == CHIP else (sources[4], sources[3], p + 1)
            halves = [(mine.at[p - 1], span(group)), (other.at[at], span(1 - group))]
        for q in range(2):
            pltpu.make_async_copy(
                halves[q][0], held.at[p, slot, halves[q][1]], held_sem.at[p, slot, q]
            ).start()

    def start_kinds(kinds, sources):
        for p in (1, 2, 0):
            for slot, kind in enumerate(kinds):
                start(kind, p, slot, sources)

    if mode == "whole":
        start_kinds((OWN, CORE, CHIP, BOTH), weights[0])
    else:
        for match in range(2):
            kinds = (OWN, CHIP) if match == (mode == "first") else (CORE, BOTH)
            for s in range(sections):
                here = jnp.logical_and(meta[MATCH] == match, meta[SECOND] == s)
                pl.when(here)(partial(start_kinds, kinds, weights[s]))

    square = jnp.zeros((tokens, 1), jnp.float32)
    for k in range(slots):
        if mode == "whole":
            piece = pieces[0][:, k * width : (k + 1) * width]
            hidden[k] = piece
        else:
            piece = pieces[k][...]
            hidden[1 - meta[SAME] if k == 0 else meta[SAME]] = piece
        wide = piece.astype(jnp.float32)
        square = square + jnp.sum(wide * wide, axis=1, keepdims=True)
    if mode == "last":
        square = square + earlier_square[:, :1]
    if mode == "first":
        out_ref2[...] = jnp.broadcast_to(square, out_ref2.shape)
    else:
        scale = lax.rsqrt(square / (4 * width) + 1e-05)

    for p in (1, 2, 0):
        for slot in range(slots):
            for q in range(2):
                pltpu.make_async_copy(
                    own_in.at[0, 0, pl.ds(0, part)],
                    held.at[p, slot, pl.ds(0, part)],
                    held_sem.at[p, slot, q],
                ).wait()
            at = meta[ROW + slot] if mode == "whole" else slot
            product = jnp.dot(hidden[at], held[p, slot], preferred_element_type=jnp.float32)
            if slot > 0:
                total[p] += product
            elif mode == "last":
                total[p] = earlier[p] + product
            else:
                total[p] = product
    if mode == "first":
        out_ref[...] = total[...]
    else:
        out_ref[...] = (total[0] * scale).astype(out_ref.dtype)
        out_ref2[...] = ((total[1] * scale) * (total[2] * scale)).astype(out_ref2.dtype)


def project_in(mode, step, plan, pieces, earlier, own_in, core_in, weights):
    width, channels = own_in.shape[2:]
    tokens = pieces[0].shape[0]
    sections = len(weights)
    slots = 4 if mode == "whole" else 2
    anywhere = pl.BlockSpec(memory_space=pl.ANY)
    vmem = pl.BlockSpec(memory_space=pltpu.VMEM)
    smem = pl.BlockSpec(memory_space=pltpu.SMEM)
    if mode == "first":
        out = (
            jax.ShapeDtypeStruct((3, tokens, channels), jnp.float32),
            jax.ShapeDtypeStruct((tokens, 128), jnp.float32),
        )
    else:
        out = (jax.ShapeDtypeStruct((tokens, channels), jnp.bfloat16),) * 2
    return pl.pallas_call(
        partial(in_kernel, mode, step, sections),
        out_shape=out,
        in_specs=[smem]
        + [vmem] * (len(pieces) + len(earlier))
        + [anywhere] * (2 + sum(len(w) for w in weights)),
        out_specs=(vmem, vmem),
        scratch_shapes=[
            pltpu.VMEM((slots, tokens, width), jnp.bfloat16),
            pltpu.VMEM((3, slots, width, channels), jnp.bfloat16),
            pltpu.VMEM((3, tokens, channels), jnp.float32),
            pltpu.SemaphoreType.DMA((3, slots, 2)),
        ],
        compiler_params=pltpu.CompilerParams(vmem_limit_bytes=44 * MIB),
        cost_estimate=pl.CostEstimate(
            flops=6 * slots * tokens * width * channels,
            bytes_accessed=6 * slots * width * channels,
            transcendentals=0,
        ),
        name="project_in_" + mode,
    )(plan, *pieces, *earlier, own_in, core_in, *[w for ws in weights for w in ws])


BLOCK = 64


def filter_kernel(step, plan, halo, mixed, query, bands, short, gated, extended):
    reach, tokens = halo.shape[0], mixed.shape[0]
    channels = mixed.shape[1]
    group_size = channels // (bands.shape[0] // BLOCK)

    @pl.when(plan[step] == 0)
    def _():
        extended[:reach] = halo[...].astype(jnp.float32)
        extended[reach:] = mixed[...].astype(jnp.float32)
        taps = short[...].astype(jnp.float32)
        total = jnp.zeros((tokens, channels), jnp.float32)
        for t in range(taps.shape[0]):
            total = total + taps[t : t + 1] * extended[reach - t : reach - t + tokens]
        gated[...] = (query[...].astype(jnp.float32) * total).astype(gated.dtype)

    @pl.when(plan[step] != 0)
    def _():
        lanes = 128
        per_tile = lanes // group_size
        lane_group = lax.broadcasted_iota(jnp.int32, (BLOCK, lanes), 1) // group_size
        for tile in range(channels // lanes):
            at = slice(tile * lanes, (tile + 1) * lanes)
            column = jnp.concatenate([halo[:, at], mixed[:, at]], 0)
            band = bands[tile * per_tile * BLOCK : (tile + 1) * per_tile * BLOCK]
            for b in range(tokens // BLOCK):
                window = column[b * BLOCK : b * BLOCK + reach + BLOCK]
                product = jnp.dot(band, window, preferred_element_type=jnp.float32)
                total = product[:BLOCK]
                for m in range(1, per_tile):
                    total = jnp.where(
                        lane_group == m, product[m * BLOCK : (m + 1) * BLOCK], total
                    )
                rows = slice(b * BLOCK, (b + 1) * BLOCK)
                gated[rows, at] = (query[rows, at].astype(jnp.float32) * total).astype(gated.dtype)


def filter_and_gate(step, plan, halo, mixed, query, bands, short):
    tokens, channels = mixed.shape
    vmem = pl.BlockSpec(memory_space=pltpu.VMEM)
    return pl.pallas_call(
        partial(filter_kernel, step),
        out_shape=jax.ShapeDtypeStruct(mixed.shape, jnp.bfloat16),
        in_specs=[pl.BlockSpec(memory_space=pltpu.SMEM)] + [vmem] * 5,
        out_specs=vmem,
        scratch_shapes=[pltpu.VMEM((halo.shape[0] + tokens, channels), jnp.float32)],
        compiler_params=pltpu.CompilerParams(vmem_limit_bytes=8 * MIB),
        cost_estimate=pl.CostEstimate(
            flops=2 * tokens * channels * 1024, bytes_accessed=8 * tokens * channels, transcendentals=0
        ),
        name="filter_and_gate",
    )(plan, halo, mixed, query, bands, short)


def tap_bands(medium_taps):
    reach, groups = medium_taps.shape
    length = 2 * reach
    zero = jnp.zeros((groups, 1), medium_taps.dtype)
    tail = jnp.zeros((groups, reach - 1), medium_taps.dtype)
    cycle = jnp.concatenate([zero, medium_taps[::-1].T, tail], 1)
    skewed = jnp.broadcast_to(cycle[:, None], (groups, BLOCK, length)).reshape(groups, -1)
    skewed = skewed[:, : BLOCK * (length - 1)].reshape(groups, BLOCK, length - 1)
    return skewed[:, :, : reach + BLOCK].reshape(groups * BLOCK, reach + BLOCK)


def out_kernel(step, sections, plan, *refs):
    meta = scalars(plan, step)
    own_gated, core_gated, own_hidden, core_hidden = refs[:4]
    weights = [refs[4 + 5 * s : 9 + 5 * s] for s in range(sections)]
    own_out, core_out, held, held_sem = refs[4 + 5 * sections :]
    tokens, width = own_hidden.shape
    part = width // 2
    group = meta[GROUP]
    mine = pl.ds(pl.multiple_of(group * part, part), part)
    other = pl.ds(pl.multiple_of((1 - group) * part, part), part)

    def start(first, second):
        for k in range(4):
            pltpu.make_async_copy(first.at[k], held.at[k, mine], held_sem.at[k, 0]).start()
            pltpu.make_async_copy(second.at[k], held.at[k, other], held_sem.at[k, 1]).start()

    for s in range(sections):
        shard, same_mine, same_other, cross_mine, cross_other = weights[s]
        cases = (
            (meta[SAME] == 0, cross_mine, cross_other),
            (meta[SAME] + meta[MATCH] == 2, shard, same_other),
            (meta[SAME] - meta[MATCH] == 1, same_mine, same_other),
        )
        for here, first, second in cases:
            if sections > 1:
                here = jnp.logical_and(here, meta[SECOND] == s)
            pl.when(here)(partial(start, first, second))

    total = None
    for k in range(4):
        for n, at in enumerate((mine, other)):
            pltpu.make_async_copy(weights[0][0].at[0], held.at[k, at], held_sem.at[k, n]).wait()
        both = jnp.concatenate([own_gated[k], core_gated[k]], 0)
        product = lax.dot_general(
            both, held[k], (((1,), (1,)), ((), ())), preferred_element_type=jnp.float32
        )
        total = product if total is None else total + product
    own_out[...] = (own_hidden[...].astype(jnp.float32) + total[:tokens]).astype(own_out.dtype)
    core_out[...] = (core_hidden[...].astype(jnp.float32) + total[tokens:]).astype(core_out.dtype)


def project_out(step, plan, own_gated, core_gated, own_hidden, core_hidden, weights):
    tokens, width = own_hidden.shape
    channels = own_gated.shape[2]
    sections = len(weights)
    anywhere = pl.BlockSpec(memory_space=pl.ANY)
    vmem = pl.BlockSpec(memory_space=pltpu.VMEM)
    smem = pl.BlockSpec(memory_space=pltpu.SMEM)
    out = jax.ShapeDtypeStruct((tokens, width), jnp.bfloat16)
    return pl.pallas_call(
        partial(out_kernel, step, sections),
        out_shape=(out, out),
        in_specs=[smem] + [vmem] * 4 + [anywhere] * (5 * sections),
        out_specs=(vmem, vmem),
        scratch_shapes=[
            pltpu.VMEM((4, width, channels), jnp.bfloat16),
            pltpu.SemaphoreType.DMA((4, 2)),
        ],
        compiler_params=pltpu.CompilerParams(vmem_limit_bytes=16 * MIB),
        cost_estimate=pl.CostEstimate(
            flops=16 * tokens * width * channels,
            bytes_accessed=8 * width * channels,
            transcendentals=0,
        ),
        name="project_out",
    )(plan, own_gated, core_gated, own_hidden, core_hidden, *[w for ws in weights for w in ws])


def taken_kernel(second, runs, plan, in_ref, out_ref, *refs):
    outs, sem = refs[:-1], refs[-1]
    section = 1 - plan[0] if second else plan[0]
    group = lax.axis_index("groups")
    part = outs[0].shape[0]
    mine = pl.ds(pl.multiple_of(group * part, part), part)
    pairs = [(out_ref.at[section, mine], outs[0])]
    for run, out in zip(runs, outs[1:]):
        for n, (p, q) in enumerate(run):
            pairs.append((in_ref.at[section, p, mine if q is None else pl.ds(q * part, part)], out.at[n]))
    copies = [pltpu.make_async_copy(*pair, sem.at[n]) for n, pair in enumerate(pairs)]
    for copy in copies[1:] + copies[:1]:
        copy.start()
    for copy in copies:
        copy.wait()


def taken(second, runs, plan, in_weights, out_weights):
    part, channels = out_weights.shape[1] // 2, out_weights.shape[2]
    far = pl.BlockSpec(memory_space=pltpu.HBM)
    near = pl.BlockSpec(memory_space=pltpu.VMEM)
    shapes = [(part, channels)] + [(len(run), part, channels) for run in runs]
    return pl.pallas_call(
        partial(taken_kernel, second, runs),
        out_shape=tuple(jax.ShapeDtypeStruct(shape, jnp.bfloat16) for shape in shapes),
        in_specs=[pl.BlockSpec(memory_space=pltpu.SMEM), far, far],
        out_specs=(near,) * len(shapes),
        scratch_shapes=[pltpu.SemaphoreType.DMA((5,))],
        compiler_params=pltpu.CompilerParams(vmem_limit_bytes=8 * MIB),
        name="taken",
    )(plan, in_weights, out_weights)


def after(value, *others):
    return lax.optimization_barrier((value,) + others)[0]


EVERY = ("groups", "ctx", "chan")
PLANE = ("ctx", "chan")


class Rounds:
    def __init__(self):
        self.before, self.now = [], []

    def __call__(self, value, axes, pairs):
        return self.join(after(value, *self.before) if self.before else value, axes, pairs)

    def join(self, value, axes, pairs):
        self.now.append(lax.ppermute(value, axes, pairs))
        return self.now[-1]

    def turn(self):
        self.before, self.now = self.now, []


def holder(x, j):
    return 2 * x + j % 2


def keeper(x, j):
    return 3 * x


def other_keeper(x, j):
    return 2 - x


def plane_pairs(source, target):
    return [(flat(source(x, j), j), flat(target(x, j), j)) for x in range(2) for j in range(4)]


def group_pairs(source, target):
    return [
        (flat(source(x, j), j, q), flat(target(x, j), j, 1 - q))
        for x in range(2)
        for j in range(4)
        for q in range(2)
    ]


CORES = ctx_pairs(1)
CHIPS = ctx_pairs(2)
GROUPS = [(0, 1), (1, 0)]
ALONG = {
    k: [(flat(holder(x, j), (j - k) % 4), flat(holder(x, j), j)) for x in range(2) for j in range(4)]
    for k in (1, 2, 3)
}
TO_KEEPER = [pair for pair in plane_pairs(holder, keeper) if pair[0] != pair[1]]
TO_OTHER_KEEPER = plane_pairs(holder, other_keeper)
TO_KEEPER_OVER = group_pairs(holder, keeper)
OTHER_KEEPERS_OVER = group_pairs(other_keeper, other_keeper)
BESIDE = [(s, s ^ 1) for s in range(4)]
HALO = [(0, 1), (1, 2), (2, 3)]


def around(k):
    return [(s, (s + k) % 4) for s in range(4)]


def shards(stream, in_weights, out_weights, short_taps, medium_taps, plan):
    g, i, j = lax.axis_index("groups"), lax.axis_index("ctx"), lax.axis_index("chan")
    x, c, h = i // 2, i % 2, j % 2
    reach = medium_taps.shape[0]
    width = stream.shape[1]
    part = width // 2
    in_weights = in_weights.transpose(0, 2, 1, 3)
    near = (j // 2) == c
    send = Rounds()

    whole = lax.all_gather(stream, "chan", axis=1, tiled=True)
    send.now.append(whole)
    out_a, all_a = taken(False, (((0, None), (1, None), (2, None)),), plan, in_weights, out_weights)
    x_a = send(all_a, "ctx", CHIPS)
    core_in = send(after(in_weights, all_a), "ctx", CORES)
    runs = (((1, None), (2, None)), ((0, 0), (0, 1)))
    out_b, kv_b, q_b = taken(True, runs, after(plan, all_a), in_weights, out_weights)
    bands = tap_bands(after(medium_taps, all_a))
    send.now += [out_b, bands]

    send.turn()
    y_a = send(x_a, "groups", GROUPS)
    x_kv_b = send(kv_b, "ctx", CHIPS)
    shard_a = [out_a] + [send(out_a, PLANE, ALONG[k]) for k in (1, 2, 3)]
    c_x = lax.ppermute(x_a, "ctx", CORES)

    send.turn()
    shard_a = jnp.stack(shard_a)
    cross_a = send(shard_a, PLANE, TO_OTHER_KEEPER)
    same_y = send(shard_a, EVERY, TO_KEEPER_OVER)
    c_y = send(y_a, "ctx", CORES)
    same_a = send(shard_a, PLANE, TO_KEEPER)
    shard_b = [out_b] + [send(after(out_b, c_y, same_a), PLANE, ALONG[k]) for k in (1, 2, 3)]

    send.turn()
    shard_b = jnp.stack(shard_b)
    cross_y = send(cross_a, EVERY, OTHER_KEEPERS_OVER)
    weights_in = [[x_a, y_a, c_x, c_y]]
    weights_out = [[shard_a, same_a, same_y, cross_a, cross_y]]

    own_hidden = lax.dynamic_slice_in_dim(whole, (2 * c + h) * width, width, 1)
    to_core = lax.dynamic_slice_in_dim(whole, (2 * (1 - c) + h) * width, width, 1)
    core_hidden = lax.ppermute(to_core, "ctx", CORES)
    inputs = in_weights, core_in

    for step in range(STEPS):
        count = 1 if step == 0 else 2
        if step == 0:
            query, mixed = project_in("whole", step, plan, [whole], [], *inputs, weights_in)
        else:
            part_sums = project_in("first", step, plan, near_pieces, [], *inputs, weights_in)
            query, mixed = project_in("last", step, plan, far_pieces, part_sums, *inputs, weights_in)
        halo = lax.ppermute(mixed[-reach:], "ctx", HALO)
        if step == 0:
            c_kv_b = lax.ppermute(after(x_kv_b, halo), "ctx", CORES)
        gated = filter_and_gate(step, plan, halo, mixed, query, bands, short_taps)
        if step == 0:
            cross_b = send(after(shard_b, halo), PLANE, TO_OTHER_KEEPER)
        g_2, g_3, g_1 = (send.join(gated, "chan", around(k)) for k in (2, 3, 1))
        if step == 0:
            send.turn()
            y_kv_b = send(x_kv_b, "groups", GROUPS)
            x_q_b = send(q_b, "ctx", CHIPS)
        own_gated = jnp.stack([gated, g_1, g_2, g_3])
        core_gated = lax.ppermute(own_gated, "ctx", CORES)
        own_hidden, core_hidden = project_out(
            step, plan, own_gated, core_gated, own_hidden, core_hidden, weights_out[:count]
        )
        swapped = lax.ppermute(core_hidden, "ctx", CORES)
        if step == STEPS - 1:
            return jnp.where((j // 2) == c, own_hidden, swapped)
        near_pieces = [own_hidden, swapped]
        far_pieces = [send.join(piece, "chan", BESIDE) for piece in near_pieces]
        if step == 0:
            send.turn()
            both_b = send(jnp.concatenate([x_q_b, y_kv_b]), "ctx", CORES)
            same_b_y = send(shard_b, EVERY, TO_KEEPER_OVER)
            same_b = send(shard_b, PLANE, TO_KEEPER)
            cross_b_y = send(cross_b, EVERY, OTHER_KEEPERS_OVER)
            weights_in.append([x_kv_b, y_kv_b, x_q_b, both_b, c_kv_b])
            weights_out.append([shard_b, same_b, same_b_y, cross_b, cross_b_y])


def solution(mesh):
    special = dict(mesh.shape) == {"groups": 2, "ctx": 4, "chan": 4}
    return jax.shard_map(
        shards if special else general_shards,
        mesh=mesh,
        in_specs=(
            P(("groups", "ctx"), "chan"),
            P(None, "ctx", None, "chan"),
            P(None, "ctx", "chan"),
            P(None, "chan"),
            P(None, "chan"),
            P(),
        ),
        out_specs=P(("groups", "ctx"), "chan"),
        check_vma=False,
    )
```

```python
from functools import partial

import jax
import jax.numpy as jnp
from jax import lax
from jax.experimental import pallas as pl
from jax.experimental.pallas import tpu as pltpu
from jax.sharding import PartitionSpec as P

STEPS = 4
MIB = 1024 * 1024


def passed_along(value, axis, steps):
    count = lax.axis_size(axis)
    leading, last = (max(0, -steps), min(count, count - steps))
    return lax.ppermute(value, axis, [(source, source + steps) for source in range(leading, last)])


def section_taps(section, short_taps, medium_taps):
    reach = medium_taps.shape[0]
    channels = short_taps.shape[1]
    padding = jnp.zeros((reach - short_taps.shape[0], channels), short_taps.dtype)
    short_full = jnp.concatenate([short_taps, padding], 0)
    group_size = channels // medium_taps.shape[1]
    medium_full = jnp.broadcast_to(
        medium_taps[:, :, None], (reach, medium_taps.shape[1], group_size)
    ).reshape(reach, channels)
    return jnp.where(section == 0, short_full, medium_full)


def causal_filter(extended, filter_taps):
    filtered = lax.conv_general_dilated(
        extended[None],
        filter_taps[::-1][:, None, :],
        (1,),
        "VALID",
        dimension_numbers=("NWC", "WIO", "NWC"),
        feature_group_count=filter_taps.shape[1],
        preferred_element_type=jnp.float32,
    )
    return filtered[0]


def filter_gate(projected, section, short_taps, medium_taps):
    query_bf = projected[:, 0].astype(jnp.bfloat16)
    mixed_bf = (projected[:, 1] * projected[:, 2]).astype(jnp.bfloat16)
    reach = medium_taps.shape[0]
    earlier = passed_along(mixed_bf[-reach:], "ctx", 1)
    extended = jnp.concatenate([earlier[1:], mixed_bf], 0)
    filtered = causal_filter(extended, section_taps(section, short_taps, medium_taps))
    return (query_bf.astype(jnp.float32) * filtered).astype(jnp.bfloat16)


def general_shards(stream, in_weights, out_weights, short_taps, medium_taps, plan):
    hidden = stream
    weights_in = lax.all_gather(in_weights, "ctx", axis=1, tiled=True)
    weights_out = lax.all_gather(out_weights, "ctx", axis=1, tiled=True)
    for step in range(STEPS):
        section = plan[step]
        full_rows = lax.all_gather(hidden, "chan", axis=1, tiled=True)
        widened = full_rows.astype(jnp.float32)
        row_scale = lax.rsqrt(jnp.mean(widened * widened, axis=1, keepdims=True) + 1e-05)
        chosen = lax.dynamic_index_in_dim(weights_in, section, 0, keepdims=False)
        projected = jnp.dot(
            full_rows, chosen.reshape(chosen.shape[0], -1), preferred_element_type=jnp.float32
        )
        projected = projected.reshape(full_rows.shape[0], 3, -1) * row_scale[:, :, None]
        gated = filter_gate(projected, section, short_taps, medium_taps)
        chosen = lax.dynamic_index_in_dim(weights_out, section, 0, keepdims=False)
        product = lax.dot_general(
            gated, chosen, (((1,), (1,)), ((), ())), preferred_element_type=jnp.float32
        )
        update = lax.psum_scatter(
            product.astype(jnp.bfloat16), "chan", scatter_dimension=1, tiled=True
        ).astype(jnp.float32)
        hidden = (hidden.astype(jnp.float32) + update).astype(jnp.bfloat16)
    return hidden


SECOND, GROUP, SAME, MATCH, ROW = range(5)


def scalars(plan, step):
    g, i, j = lax.axis_index("groups"), lax.axis_index("ctx"), lax.axis_index("chan")
    x, c, h = i >> 1, i & 1, j & 1
    second = (plan[step] != plan[0]).astype(jnp.int32)
    same, match = (x == c).astype(jnp.int32), (c == h).astype(jnp.int32)
    return [second, g, same, match, i, i ^ 1, i ^ 2, i ^ 3]


def ctx_pairs(change):
    return [(i, i ^ change) for i in range(4)]


def flat(i, j, g=None):
    return (i * 4 + j) if g is None else (g * 16 + i * 4 + j)


OWN, CORE, CHIP, BOTH = range(4)


def in_kernel(mode, step, sections, plan, *refs):
    meta = scalars(plan, step)
    section = plan[step]
    count = 1 if mode == "whole" else 2
    pieces, refs = refs[:count], refs[count:]
    if mode == "last":
        earlier, earlier_square, refs = refs[0], refs[1], refs[2:]
    own_in, core_in = refs[:2]
    weights, refs = [refs[2:6], refs[6:11]], refs[6 if sections == 1 else 11 :]
    out_ref, out_ref2, hidden, held, total, held_sem = refs
    tokens, width = hidden.shape[1:]
    part = width // 2
    group = meta[GROUP]
    slots = held.shape[1]

    def span(q):
        return pl.ds(pl.multiple_of(q * part, part), part)

    def start(kind, p, slot, sources):
        if kind in (OWN, CORE):
            source = own_in if kind == OWN else core_in
            halves = [(source.at[section, p, span(q)], span(q)) for q in range(2)]
        elif len(sources) == 4:
            mine, other = sources[:2] if kind == CHIP else sources[2:]
            halves = [(mine.at[p], span(group)), (other.at[p], span(1 - group))]
        elif p == 0:
            source = sources[2 if kind == CHIP else 3]
            halves = [(source.at[q], span(q)) for q in range(2)]
        else:
            mine, other, at = (sources[0], sources[1], p - 1) if kind == CHIP else (sources[4], sources[3], p + 1)
            halves = [(mine.at[p - 1], span(group)), (other.at[at], span(1 - group))]
        for q in range(2):
            pltpu.make_async_copy(
                halves[q][0], held.at[p, slot, halves[q][1]], held_sem.at[p, slot, q]
            ).start()

    def start_kinds(kinds, sources):
        for p in (1, 2, 0):
            for slot, kind in enumerate(kinds):
                start(kind, p, slot, sources)

    if mode == "whole":
        start_kinds((OWN, CORE, CHIP, BOTH), weights[0])
    else:
        for match in range(2):
            kinds = (OWN, CHIP) if match == (mode == "first") else (CORE, BOTH)
            for s in range(sections):
                here = jnp.logical_and(meta[MATCH] == match, meta[SECOND] == s)
                pl.when(here)(partial(start_kinds, kinds, weights[s]))

    square = jnp.zeros((tokens, 1), jnp.float32)
    for k in range(slots):
        if mode == "whole":
            piece = pieces[0][:, k * width : (k + 1) * width]
            hidden[k] = piece
        else:
            piece = pieces[k][...]
            hidden[1 - meta[SAME] if k == 0 else meta[SAME]] = piece
        wide = piece.astype(jnp.float32)
        square = square + jnp.sum(wide * wide, axis=1, keepdims=True)
    if mode == "last":
        square = square + earlier_square[:, :1]
    if mode == "first":
        out_ref2[...] = jnp.broadcast_to(square, out_ref2.shape)
    else:
        scale = lax.rsqrt(square / (4 * width) + 1e-05)

    for p in (1, 2, 0):
        for slot in range(slots):
            for q in range(2):
                pltpu.make_async_copy(
                    own_in.at[0, 0, pl.ds(0, part)],
                    held.at[p, slot, pl.ds(0, part)],
                    held_sem.at[p, slot, q],
                ).wait()
            at = meta[ROW + slot] if mode == "whole" else slot
            product = jnp.dot(hidden[at], held[p, slot], preferred_element_type=jnp.float32)
            if slot > 0:
                total[p] += product
            elif mode == "last":
                total[p] = earlier[p] + product
            else:
                total[p] = product
    if mode == "first":
        out_ref[...] = total[...]
    else:
        out_ref[...] = (total[0] * scale).astype(out_ref.dtype)
        out_ref2[...] = ((total[1] * scale) * (total[2] * scale)).astype(out_ref2.dtype)


def project_in(mode, step, plan, pieces, earlier, own_in, core_in, weights):
    width, channels = own_in.shape[2:]
    tokens = pieces[0].shape[0]
    sections = len(weights)
    slots = 4 if mode == "whole" else 2
    anywhere = pl.BlockSpec(memory_space=pl.ANY)
    vmem = pl.BlockSpec(memory_space=pltpu.VMEM)
    smem = pl.BlockSpec(memory_space=pltpu.SMEM)
    if mode == "first":
        out = (
            jax.ShapeDtypeStruct((3, tokens, channels), jnp.float32),
            jax.ShapeDtypeStruct((tokens, 128), jnp.float32),
        )
    else:
        out = (jax.ShapeDtypeStruct((tokens, channels), jnp.bfloat16),) * 2
    return pl.pallas_call(
        partial(in_kernel, mode, step, sections),
        out_shape=out,
        in_specs=[smem]
        + [vmem] * (len(pieces) + len(earlier))
        + [anywhere] * (2 + sum(len(w) for w in weights)),
        out_specs=(vmem, vmem),
        scratch_shapes=[
            pltpu.VMEM((slots, tokens, width), jnp.bfloat16),
            pltpu.VMEM((3, slots, width, channels), jnp.bfloat16),
            pltpu.VMEM((3, tokens, channels), jnp.float32),
            pltpu.SemaphoreType.DMA((3, slots, 2)),
        ],
        compiler_params=pltpu.CompilerParams(vmem_limit_bytes=44 * MIB),
        cost_estimate=pl.CostEstimate(
            flops=6 * slots * tokens * width * channels,
            bytes_accessed=6 * slots * width * channels,
            transcendentals=0,
        ),
        name="project_in_" + mode,
    )(plan, *pieces, *earlier, own_in, core_in, *[w for ws in weights for w in ws])


BLOCK = 64


def filter_kernel(step, plan, halo, mixed, query, bands, short, gated, extended):
    reach, tokens = halo.shape[0], mixed.shape[0]
    channels = mixed.shape[1]
    group_size = channels // (bands.shape[0] // BLOCK)

    @pl.when(plan[step] == 0)
    def _():
        extended[:reach] = halo[...].astype(jnp.float32)
        extended[reach:] = mixed[...].astype(jnp.float32)
        taps = short[...].astype(jnp.float32)
        total = jnp.zeros((tokens, channels), jnp.float32)
        for t in range(taps.shape[0]):
            total = total + taps[t : t + 1] * extended[reach - t : reach - t + tokens]
        gated[...] = (query[...].astype(jnp.float32) * total).astype(gated.dtype)

    @pl.when(plan[step] != 0)
    def _():
        lanes = 128
        per_tile = lanes // group_size
        lane_group = lax.broadcasted_iota(jnp.int32, (BLOCK, lanes), 1) // group_size
        for tile in range(channels // lanes):
            at = slice(tile * lanes, (tile + 1) * lanes)
            column = jnp.concatenate([halo[:, at], mixed[:, at]], 0)
            band = bands[tile * per_tile * BLOCK : (tile + 1) * per_tile * BLOCK]
            for b in range(tokens // BLOCK):
                window = column[b * BLOCK : b * BLOCK + reach + BLOCK]
                product = jnp.dot(band, window, preferred_element_type=jnp.float32)
                total = product[:BLOCK]
                for m in range(1, per_tile):
                    total = jnp.where(
                        lane_group == m, product[m * BLOCK : (m + 1) * BLOCK], total
                    )
                rows = slice(b * BLOCK, (b + 1) * BLOCK)
                gated[rows, at] = (query[rows, at].astype(jnp.float32) * total).astype(gated.dtype)


def filter_and_gate(step, plan, halo, mixed, query, bands, short):
    tokens, channels = mixed.shape
    vmem = pl.BlockSpec(memory_space=pltpu.VMEM)
    return pl.pallas_call(
        partial(filter_kernel, step),
        out_shape=jax.ShapeDtypeStruct(mixed.shape, jnp.bfloat16),
        in_specs=[pl.BlockSpec(memory_space=pltpu.SMEM)] + [vmem] * 5,
        out_specs=vmem,
        scratch_shapes=[pltpu.VMEM((halo.shape[0] + tokens, channels), jnp.float32)],
        compiler_params=pltpu.CompilerParams(vmem_limit_bytes=8 * MIB),
        cost_estimate=pl.CostEstimate(
            flops=2 * tokens * channels * 1024, bytes_accessed=8 * tokens * channels, transcendentals=0
        ),
        name="filter_and_gate",
    )(plan, halo, mixed, query, bands, short)


def tap_bands(medium_taps):
    reach, groups = medium_taps.shape
    length = 2 * reach
    zero = jnp.zeros((groups, 1), medium_taps.dtype)
    tail = jnp.zeros((groups, reach - 1), medium_taps.dtype)
    cycle = jnp.concatenate([zero, medium_taps[::-1].T, tail], 1)
    skewed = jnp.broadcast_to(cycle[:, None], (groups, BLOCK, length)).reshape(groups, -1)
    skewed = skewed[:, : BLOCK * (length - 1)].reshape(groups, BLOCK, length - 1)
    return skewed[:, :, : reach + BLOCK].reshape(groups * BLOCK, reach + BLOCK)


def out_kernel(step, sections, plan, *refs):
    meta = scalars(plan, step)
    own_gated, core_gated, own_hidden, core_hidden = refs[:4]
    weights = [refs[4 + 5 * s : 9 + 5 * s] for s in range(sections)]
    own_out, core_out, held, held_sem = refs[4 + 5 * sections :]
    tokens, width = own_hidden.shape
    part = width // 2
    group = meta[GROUP]
    mine = pl.ds(pl.multiple_of(group * part, part), part)
    other = pl.ds(pl.multiple_of((1 - group) * part, part), part)

    def start(first, second):
        for k in range(4):
            pltpu.make_async_copy(first.at[k], held.at[k, mine], held_sem.at[k, 0]).start()
            pltpu.make_async_copy(second.at[k], held.at[k, other], held_sem.at[k, 1]).start()

    for s in range(sections):
        shard, same_mine, same_other, cross_mine, cross_other = weights[s]
        cases = (
            (meta[SAME] == 0, cross_mine, cross_other),
            (meta[SAME] + meta[MATCH] == 2, shard, same_other),
            (meta[SAME] - meta[MATCH] == 1, same_mine, same_other),
        )
        for here, first, second in cases:
            if sections > 1:
                here = jnp.logical_and(here, meta[SECOND] == s)
            pl.when(here)(partial(start, first, second))

    total = None
    for k in range(4):
        for n, at in enumerate((mine, other)):
            pltpu.make_async_copy(weights[0][0].at[0], held.at[k, at], held_sem.at[k, n]).wait()
        both = jnp.concatenate([own_gated[k], core_gated[k]], 0)
        product = lax.dot_general(
            both, held[k], (((1,), (1,)), ((), ())), preferred_element_type=jnp.float32
        )
        total = product if total is None else total + product
    own_out[...] = (own_hidden[...].astype(jnp.float32) + total[:tokens]).astype(own_out.dtype)
    core_out[...] = (core_hidden[...].astype(jnp.float32) + total[tokens:]).astype(core_out.dtype)


def project_out(step, plan, own_gated, core_gated, own_hidden, core_hidden, weights):
    tokens, width = own_hidden.shape
    channels = own_gated.shape[2]
    sections = len(weights)
    anywhere = pl.BlockSpec(memory_space=pl.ANY)
    vmem = pl.BlockSpec(memory_space=pltpu.VMEM)
    smem = pl.BlockSpec(memory_space=pltpu.SMEM)
    out = jax.ShapeDtypeStruct((tokens, width), jnp.bfloat16)
    return pl.pallas_call(
        partial(out_kernel, step, sections),
        out_shape=(out, out),
        in_specs=[smem] + [vmem] * 4 + [anywhere] * (5 * sections),
        out_specs=(vmem, vmem),
        scratch_shapes=[
            pltpu.VMEM((4, width, channels), jnp.bfloat16),
            pltpu.SemaphoreType.DMA((4, 2)),
        ],
        compiler_params=pltpu.CompilerParams(vmem_limit_bytes=16 * MIB),
        cost_estimate=pl.CostEstimate(
            flops=16 * tokens * width * channels,
            bytes_accessed=8 * width * channels,
            transcendentals=0,
        ),
        name="project_out",
    )(plan, own_gated, core_gated, own_hidden, core_hidden, *[w for ws in weights for w in ws])


def taken_kernel(second, runs, plan, in_ref, out_ref, *refs):
    outs, sem = refs[:-1], refs[-1]
    section = 1 - plan[0] if second else plan[0]
    group = lax.axis_index("groups")
    part = outs[0].shape[0]
    mine = pl.ds(pl.multiple_of(group * part, part), part)
    pairs = [(out_ref.at[section, mine], outs[0])]
    for run, out in zip(runs, outs[1:]):
        for n, (p, q) in enumerate(run):
            pairs.append((in_ref.at[section, p, mine if q is None else pl.ds(q * part, part)], out.at[n]))
    copies = [pltpu.make_async_copy(*pair, sem.at[n]) for n, pair in enumerate(pairs)]
    for copy in copies[1:] + copies[:1]:
        copy.start()
    for copy in copies:
        copy.wait()


def taken(second, runs, plan, in_weights, out_weights):
    part, channels = out_weights.shape[1] // 2, out_weights.shape[2]
    far = pl.BlockSpec(memory_space=pltpu.HBM)
    near = pl.BlockSpec(memory_space=pltpu.VMEM)
    shapes = [(part, channels)] + [(len(run), part, channels) for run in runs]
    return pl.pallas_call(
        partial(taken_kernel, second, runs),
        out_shape=tuple(jax.ShapeDtypeStruct(shape, jnp.bfloat16) for shape in shapes),
        in_specs=[pl.BlockSpec(memory_space=pltpu.SMEM), far, far],
        out_specs=(near,) * len(shapes),
        scratch_shapes=[pltpu.SemaphoreType.DMA((5,))],
        compiler_params=pltpu.CompilerParams(vmem_limit_bytes=(8 if second else 56) * MIB),
        name="taken",
    )(plan, in_weights, out_weights)


def after(value, *others):
    return lax.optimization_barrier((value,) + others)[0]


EVERY = ("groups", "ctx", "chan")
PLANE = ("ctx", "chan")


class Rounds:
    def __init__(self):
        self.before, self.now = [], []

    def __call__(self, value, axes, pairs):
        return self.join(after(value, *self.before) if self.before else value, axes, pairs)

    def join(self, value, axes, pairs):
        self.now.append(lax.ppermute(value, axes, pairs))
        return self.now[-1]

    def turn(self):
        self.before, self.now = self.now, []


def holder(x, j):
    return 2 * x + j % 2


def keeper(x, j):
    return 3 * x


def other_keeper(x, j):
    return 2 - x


def plane_pairs(source, target):
    return [(flat(source(x, j), j), flat(target(x, j), j)) for x in range(2) for j in range(4)]


def group_pairs(source, target):
    return [
        (flat(source(x, j), j, q), flat(target(x, j), j, 1 - q))
        for x in range(2)
        for j in range(4)
        for q in range(2)
    ]


CORES = ctx_pairs(1)
CHIPS = ctx_pairs(2)
GROUPS = [(0, 1), (1, 0)]
ALONG = {
    k: [(flat(holder(x, j), (j - k) % 4), flat(holder(x, j), j)) for x in range(2) for j in range(4)]
    for k in (1, 2, 3)
}
TO_KEEPER = [pair for pair in plane_pairs(holder, keeper) if pair[0] != pair[1]]
TO_OTHER_KEEPER = plane_pairs(holder, other_keeper)
TO_KEEPER_OVER = group_pairs(holder, keeper)
OTHER_KEEPERS_OVER = group_pairs(other_keeper, other_keeper)
BESIDE = [(s, s ^ 1) for s in range(4)]
HALO = [(0, 1), (1, 2), (2, 3)]


def around(k):
    return [(s, (s + k) % 4) for s in range(4)]


def shards(stream, in_weights, out_weights, short_taps, medium_taps, plan):
    g, i, j = lax.axis_index("groups"), lax.axis_index("ctx"), lax.axis_index("chan")
    x, c, h = i // 2, i % 2, j % 2
    reach = medium_taps.shape[0]
    width = stream.shape[1]
    part = width // 2
    in_weights = in_weights.transpose(0, 2, 1, 3)
    near = (j // 2) == c
    send = Rounds()

    whole = lax.all_gather(stream, "chan", axis=1, tiled=True)
    send.now.append(whole)
    out_a, all_a = taken(False, (((0, None), (1, None), (2, None)),), plan, in_weights, out_weights)
    x_a = send(all_a, "ctx", CHIPS)
    core_in = send(after(in_weights, all_a), "ctx", CORES)
    runs = (((1, None), (2, None)), ((0, 0), (0, 1)))
    out_b, kv_b, q_b = taken(True, runs, after(plan, all_a), in_weights, out_weights)
    bands = tap_bands(after(medium_taps, all_a))
    send.now += [out_b, bands]

    send.turn()
    y_a = send(x_a, "groups", GROUPS)
    x_kv_b = send(kv_b, "ctx", CHIPS)
    shard_a = [out_a] + [send(out_a, PLANE, ALONG[k]) for k in (1, 2, 3)]
    c_x = lax.ppermute(x_a, "ctx", CORES)

    send.turn()
    shard_a = jnp.stack(shard_a)
    cross_a = send(shard_a, PLANE, TO_OTHER_KEEPER)
    same_y = send(shard_a, EVERY, TO_KEEPER_OVER)
    c_y = send(y_a, "ctx", CORES)
    same_a = send(shard_a, PLANE, TO_KEEPER)
    shard_b = [out_b] + [send(after(out_b, c_y, same_a), PLANE, ALONG[k]) for k in (1, 2, 3)]

    send.turn()
    shard_b = jnp.stack(shard_b)
    cross_y = send.join(cross_a, EVERY, OTHER_KEEPERS_OVER)
    weights_in = [[x_a, y_a, c_x, c_y]]
    weights_out = [[shard_a, same_a, same_y, cross_a, cross_y]]

    own_hidden = lax.dynamic_slice_in_dim(whole, (2 * c + h) * width, width, 1)
    to_core = lax.dynamic_slice_in_dim(whole, (2 * (1 - c) + h) * width, width, 1)
    core_hidden = lax.ppermute(to_core, "ctx", CORES)
    inputs = in_weights, core_in

    for step in range(STEPS):
        count = 1 if step == 0 else 2
        if step == 0:
            query, mixed = project_in("whole", step, plan, [whole], [], *inputs, weights_in)
        else:
            part_sums = project_in("first", step, plan, near_pieces, [], *inputs, weights_in)
            query, mixed = project_in("last", step, plan, far_pieces, part_sums, *inputs, weights_in)
        halo = lax.ppermute(mixed[-reach:], "ctx", HALO)
        if step == 0:
            c_kv_b = lax.ppermute(after(x_kv_b, halo), "ctx", CORES)
        gated = filter_and_gate(step, plan, halo, mixed, query, bands, short_taps)
        if step == 0:
            cross_b = send(after(shard_b, halo), PLANE, TO_OTHER_KEEPER)
        g_2, g_3, g_1 = (send.join(gated, "chan", around(k)) for k in (2, 3, 1))
        if step == 0:
            send.turn()
            y_kv_b = send.join(after(x_kv_b, cross_y), "groups", GROUPS)
            x_q_b = send(q_b, "ctx", CHIPS)
            same_b_y = lax.ppermute(after(shard_b, *send.before), EVERY, TO_KEEPER_OVER)
        own_gated = jnp.stack([gated, g_1, g_2, g_3])
        core_gated = lax.ppermute(own_gated, "ctx", CORES)
        own_hidden, core_hidden = project_out(
            step, plan, own_gated, core_gated, own_hidden, core_hidden, weights_out[:count]
        )
        swapped = lax.ppermute(core_hidden, "ctx", CORES)
        if step == STEPS - 1:
            return jnp.where((j // 2) == c, own_hidden, swapped)
        near_pieces = [own_hidden, swapped]
        beside_core = send.join(core_hidden, "chan", BESIDE)
        far_pieces = [send.join(own_hidden, "chan", BESIDE), lax.ppermute(beside_core, "ctx", CORES)]
        if step == 0:
            send.turn()
            both_b = send(jnp.concatenate([x_q_b, y_kv_b]), "ctx", CORES)
            same_b = send(shard_b, PLANE, TO_KEEPER)
            cross_b_y = send(cross_b, EVERY, OTHER_KEEPERS_OVER)
            weights_in.append([x_kv_b, y_kv_b, x_q_b, both_b, c_kv_b])
            weights_out.append([shard_b, same_b, same_b_y, cross_b, cross_b_y])


def solution(mesh):
    special = dict(mesh.shape) == {"groups": 2, "ctx": 4, "chan": 4}
    return jax.shard_map(
        shards if special else general_shards,
        mesh=mesh,
        in_specs=(
            P(("groups", "ctx"), "chan"),
            P(None, "ctx", None, "chan"),
            P(None, "ctx", "chan"),
            P(None, "chan"),
            P(None, "chan"),
            P(),
        ),
        out_specs=P(("groups", "ctx"), "chan"),
        check_vma=False,
    )
```

```python
from functools import partial

import jax
import jax.numpy as jnp
from jax import lax
from jax.experimental import pallas as pl
from jax.experimental.pallas import tpu as pltpu
from jax.sharding import PartitionSpec as P

STEPS = 4
MIB = 1024 * 1024


def passed_along(value, axis, steps):
    count = lax.axis_size(axis)
    leading, last = (max(0, -steps), min(count, count - steps))
    return lax.ppermute(value, axis, [(source, source + steps) for source in range(leading, last)])


def section_taps(section, short_taps, medium_taps):
    reach = medium_taps.shape[0]
    channels = short_taps.shape[1]
    padding = jnp.zeros((reach - short_taps.shape[0], channels), short_taps.dtype)
    short_full = jnp.concatenate([short_taps, padding], 0)
    group_size = channels // medium_taps.shape[1]
    medium_full = jnp.broadcast_to(
        medium_taps[:, :, None], (reach, medium_taps.shape[1], group_size)
    ).reshape(reach, channels)
    return jnp.where(section == 0, short_full, medium_full)


def causal_filter(extended, filter_taps):
    filtered = lax.conv_general_dilated(
        extended[None],
        filter_taps[::-1][:, None, :],
        (1,),
        "VALID",
        dimension_numbers=("NWC", "WIO", "NWC"),
        feature_group_count=filter_taps.shape[1],
        preferred_element_type=jnp.float32,
    )
    return filtered[0]


def filter_gate(projected, section, short_taps, medium_taps):
    query_bf = projected[:, 0].astype(jnp.bfloat16)
    mixed_bf = (projected[:, 1] * projected[:, 2]).astype(jnp.bfloat16)
    reach = medium_taps.shape[0]
    earlier = passed_along(mixed_bf[-reach:], "ctx", 1)
    extended = jnp.concatenate([earlier[1:], mixed_bf], 0)
    filtered = causal_filter(extended, section_taps(section, short_taps, medium_taps))
    return (query_bf.astype(jnp.float32) * filtered).astype(jnp.bfloat16)


def general_shards(stream, in_weights, out_weights, short_taps, medium_taps, plan):
    hidden = stream
    weights_in = lax.all_gather(in_weights, "ctx", axis=1, tiled=True)
    weights_out = lax.all_gather(out_weights, "ctx", axis=1, tiled=True)
    for step in range(STEPS):
        section = plan[step]
        full_rows = lax.all_gather(hidden, "chan", axis=1, tiled=True)
        widened = full_rows.astype(jnp.float32)
        row_scale = lax.rsqrt(jnp.mean(widened * widened, axis=1, keepdims=True) + 1e-05)
        chosen = lax.dynamic_index_in_dim(weights_in, section, 0, keepdims=False)
        projected = jnp.dot(
            full_rows, chosen.reshape(chosen.shape[0], -1), preferred_element_type=jnp.float32
        )
        projected = projected.reshape(full_rows.shape[0], 3, -1) * row_scale[:, :, None]
        gated = filter_gate(projected, section, short_taps, medium_taps)
        chosen = lax.dynamic_index_in_dim(weights_out, section, 0, keepdims=False)
        product = lax.dot_general(
            gated, chosen, (((1,), (1,)), ((), ())), preferred_element_type=jnp.float32
        )
        update = lax.psum_scatter(
            product.astype(jnp.bfloat16), "chan", scatter_dimension=1, tiled=True
        ).astype(jnp.float32)
        hidden = (hidden.astype(jnp.float32) + update).astype(jnp.bfloat16)
    return hidden


SECOND, GROUP, SAME, MATCH, ROW = range(5)


def scalars(plan, step):
    g, i, j = lax.axis_index("groups"), lax.axis_index("ctx"), lax.axis_index("chan")
    x, c, h = i >> 1, i & 1, j & 1
    second = (plan[step] != plan[0]).astype(jnp.int32)
    same, match = (x == c).astype(jnp.int32), (c == h).astype(jnp.int32)
    return [second, g, same, match, i, i ^ 1, i ^ 2, i ^ 3]


def ctx_pairs(change):
    return [(i, i ^ change) for i in range(4)]


def flat(i, j, g=None):
    return (i * 4 + j) if g is None else (g * 16 + i * 4 + j)


OWN, CORE, CHIP, BOTH = range(4)


def in_kernel(mode, step, sections, plan, *refs):
    meta = scalars(plan, step)
    section = plan[step]
    count = 1 if mode == "whole" else 2
    pieces, refs = refs[:count], refs[count:]
    if mode == "last":
        earlier, earlier_square, refs = refs[0], refs[1], refs[2:]
    own_in, core_in = refs[:2]
    weights, refs = [refs[2:8], refs[8:13]], refs[8 if sections == 1 else 13 :]
    out_ref, out_ref2, hidden, held, total, held_sem = refs
    tokens, width = hidden.shape[1:]
    part = width // 2
    group = meta[GROUP]
    slots = held.shape[1]

    def span(q):
        return pl.ds(pl.multiple_of(q * part, part), part)

    def start(kind, p, slot, sources):
        if kind in (OWN, CORE):
            source = own_in if kind == OWN else core_in
            halves = [(source.at[section, p, span(q)], span(q)) for q in range(2)]
        elif len(sources) == 6:
            if kind == BOTH:
                mine, other, at = sources[4], sources[5], p
            else:
                mine, other, at = (sources[2], sources[3], 0) if p == 0 else (sources[0], sources[1], p - 1)
            halves = [(mine.at[at], span(group)), (other.at[at], span(1 - group))]
        elif p == 0:
            source = sources[2 if kind == CHIP else 3]
            halves = [(source.at[q], span(q)) for q in range(2)]
        else:
            mine, other, at = (sources[0], sources[1], p - 1) if kind == CHIP else (sources[4], sources[3], p + 1)
            halves = [(mine.at[p - 1], span(group)), (other.at[at], span(1 - group))]
        for q in range(2):
            pltpu.make_async_copy(
                halves[q][0], held.at[p, slot, halves[q][1]], held_sem.at[p, slot, q]
            ).start()

    def start_kinds(kinds, sources):
        for p in (1, 2, 0):
            for slot, kind in enumerate(kinds):
                start(kind, p, slot, sources)

    if mode == "whole":
        start_kinds((OWN, CORE, CHIP, BOTH), weights[0])
    else:
        for match in range(2):
            kinds = (OWN, CHIP) if match == (mode == "first") else (CORE, BOTH)
            for s in range(sections):
                here = jnp.logical_and(meta[MATCH] == match, meta[SECOND] == s)
                pl.when(here)(partial(start_kinds, kinds, weights[s]))

    square = jnp.zeros((tokens, 1), jnp.float32)
    for k in range(slots):
        if mode == "whole":
            piece = pieces[0][:, k * width : (k + 1) * width]
            hidden[k] = piece
        else:
            piece = pieces[k][...]
            hidden[1 - meta[SAME] if k == 0 else meta[SAME]] = piece
        wide = piece.astype(jnp.float32)
        square = square + jnp.sum(wide * wide, axis=1, keepdims=True)
    if mode == "last":
        square = square + earlier_square[:, :1]
    if mode == "first":
        out_ref2[...] = jnp.broadcast_to(square, out_ref2.shape)
    else:
        scale = lax.rsqrt(square / (4 * width) + 1e-05)

    for p in (1, 2, 0):
        for slot in range(slots):
            for q in range(2):
                pltpu.make_async_copy(
                    own_in.at[0, 0, pl.ds(0, part)],
                    held.at[p, slot, pl.ds(0, part)],
                    held_sem.at[p, slot, q],
                ).wait()
            at = meta[ROW + slot] if mode == "whole" else slot
            product = jnp.dot(hidden[at], held[p, slot], preferred_element_type=jnp.float32)
            if slot > 0:
                total[p] += product
            elif mode == "last":
                total[p] = earlier[p] + product
            else:
                total[p] = product
    if mode == "first":
        out_ref[...] = total[...]
    else:
        out_ref[...] = (total[0] * scale).astype(out_ref.dtype)
        out_ref2[...] = ((total[1] * scale) * (total[2] * scale)).astype(out_ref2.dtype)


def project_in(mode, step, plan, pieces, earlier, own_in, core_in, weights):
    width, channels = own_in.shape[2:]
    tokens = pieces[0].shape[0]
    sections = len(weights)
    slots = 4 if mode == "whole" else 2
    anywhere = pl.BlockSpec(memory_space=pl.ANY)
    vmem = pl.BlockSpec(memory_space=pltpu.VMEM)
    smem = pl.BlockSpec(memory_space=pltpu.SMEM)
    if mode == "first":
        out = (
            jax.ShapeDtypeStruct((3, tokens, channels), jnp.float32),
            jax.ShapeDtypeStruct((tokens, 128), jnp.float32),
        )
    else:
        out = (jax.ShapeDtypeStruct((tokens, channels), jnp.bfloat16),) * 2
    return pl.pallas_call(
        partial(in_kernel, mode, step, sections),
        out_shape=out,
        in_specs=[smem]
        + [vmem] * (len(pieces) + len(earlier))
        + [anywhere] * (2 + sum(len(w) for w in weights)),
        out_specs=(vmem, vmem),
        scratch_shapes=[
            pltpu.VMEM((slots, tokens, width), jnp.bfloat16),
            pltpu.VMEM((3, slots, width, channels), jnp.bfloat16),
            pltpu.VMEM((3, tokens, channels), jnp.float32),
            pltpu.SemaphoreType.DMA((3, slots, 2)),
        ],
        compiler_params=pltpu.CompilerParams(vmem_limit_bytes=44 * MIB),
        cost_estimate=pl.CostEstimate(
            flops=6 * slots * tokens * width * channels,
            bytes_accessed=6 * slots * width * channels,
            transcendentals=0,
        ),
        name="project_in_" + mode,
    )(plan, *pieces, *earlier, own_in, core_in, *[w for ws in weights for w in ws])


BLOCK = 64


def filter_kernel(step, plan, halo, mixed, query, bands, short, gated, extended):
    reach, tokens = halo.shape[0], mixed.shape[0]
    channels = mixed.shape[1]
    group_size = channels // (bands.shape[0] // BLOCK)

    @pl.when(plan[step] == 0)
    def _():
        extended[:reach] = halo[...].astype(jnp.float32)
        extended[reach:] = mixed[...].astype(jnp.float32)
        taps = short[...].astype(jnp.float32)
        total = jnp.zeros((tokens, channels), jnp.float32)
        for t in range(taps.shape[0]):
            total = total + taps[t : t + 1] * extended[reach - t : reach - t + tokens]
        gated[...] = (query[...].astype(jnp.float32) * total).astype(gated.dtype)

    @pl.when(plan[step] != 0)
    def _():
        lanes = 128
        per_tile = lanes // group_size
        lane_group = lax.broadcasted_iota(jnp.int32, (BLOCK, lanes), 1) // group_size
        for tile in range(channels // lanes):
            at = slice(tile * lanes, (tile + 1) * lanes)
            column = jnp.concatenate([halo[:, at], mixed[:, at]], 0)
            band = bands[tile * per_tile * BLOCK : (tile + 1) * per_tile * BLOCK]
            for b in range(tokens // BLOCK):
                window = column[b * BLOCK : b * BLOCK + reach + BLOCK]
                product = jnp.dot(band, window, preferred_element_type=jnp.float32)
                total = product[:BLOCK]
                for m in range(1, per_tile):
                    total = jnp.where(
                        lane_group == m, product[m * BLOCK : (m + 1) * BLOCK], total
                    )
                rows = slice(b * BLOCK, (b + 1) * BLOCK)
                gated[rows, at] = (query[rows, at].astype(jnp.float32) * total).astype(gated.dtype)


def filter_and_gate(step, plan, halo, mixed, query, bands, short):
    tokens, channels = mixed.shape
    vmem = pl.BlockSpec(memory_space=pltpu.VMEM)
    return pl.pallas_call(
        partial(filter_kernel, step),
        out_shape=jax.ShapeDtypeStruct(mixed.shape, jnp.bfloat16),
        in_specs=[pl.BlockSpec(memory_space=pltpu.SMEM)] + [vmem] * 5,
        out_specs=vmem,
        scratch_shapes=[pltpu.VMEM((halo.shape[0] + tokens, channels), jnp.float32)],
        compiler_params=pltpu.CompilerParams(vmem_limit_bytes=8 * MIB),
        cost_estimate=pl.CostEstimate(
            flops=2 * tokens * channels * 1024, bytes_accessed=8 * tokens * channels, transcendentals=0
        ),
        name="filter_and_gate",
    )(plan, halo, mixed, query, bands, short)


def tap_bands(medium_taps):
    reach, groups = medium_taps.shape
    length = 2 * reach
    zero = jnp.zeros((groups, 1), medium_taps.dtype)
    tail = jnp.zeros((groups, reach - 1), medium_taps.dtype)
    cycle = jnp.concatenate([zero, medium_taps[::-1].T, tail], 1)
    skewed = jnp.broadcast_to(cycle[:, None], (groups, BLOCK, length)).reshape(groups, -1)
    skewed = skewed[:, : BLOCK * (length - 1)].reshape(groups, BLOCK, length - 1)
    return skewed[:, :, : reach + BLOCK].reshape(groups * BLOCK, reach + BLOCK)


def out_kernel(step, sections, plan, *refs):
    meta = scalars(plan, step)
    own_gated, core_gated, own_hidden, core_hidden = refs[:4]
    weights = [refs[4 + 5 * s : 9 + 5 * s] for s in range(sections)]
    own_out, core_out, held, held_sem = refs[4 + 5 * sections :]
    tokens, width = own_hidden.shape
    part = width // 2
    group = meta[GROUP]
    mine = pl.ds(pl.multiple_of(group * part, part), part)
    other = pl.ds(pl.multiple_of((1 - group) * part, part), part)

    def start(first, second):
        for k in range(4):
            pltpu.make_async_copy(first.at[k], held.at[k, mine], held_sem.at[k, 0]).start()
            pltpu.make_async_copy(second.at[k], held.at[k, other], held_sem.at[k, 1]).start()

    for s in range(sections):
        shard, same_mine, same_other, cross_mine, cross_other = weights[s]
        cases = (
            (meta[SAME] == 0, cross_mine, cross_other),
            (meta[SAME] + meta[MATCH] == 2, shard, same_other),
            (meta[SAME] - meta[MATCH] == 1, same_mine, same_other),
        )
        for here, first, second in cases:
            if sections > 1:
                here = jnp.logical_and(here, meta[SECOND] == s)
            pl.when(here)(partial(start, first, second))

    total = None
    for k in range(4):
        for n, at in enumerate((mine, other)):
            pltpu.make_async_copy(weights[0][0].at[0], held.at[k, at], held_sem.at[k, n]).wait()
        both = jnp.concatenate([own_gated[k], core_gated[k]], 0)
        product = lax.dot_general(
            both, held[k], (((1,), (1,)), ((), ())), preferred_element_type=jnp.float32
        )
        total = product if total is None else total + product
    own_out[...] = (own_hidden[...].astype(jnp.float32) + total[:tokens]).astype(own_out.dtype)
    core_out[...] = (core_hidden[...].astype(jnp.float32) + total[tokens:]).astype(core_out.dtype)


def project_out(step, plan, own_gated, core_gated, own_hidden, core_hidden, weights):
    tokens, width = own_hidden.shape
    channels = own_gated.shape[2]
    sections = len(weights)
    anywhere = pl.BlockSpec(memory_space=pl.ANY)
    vmem = pl.BlockSpec(memory_space=pltpu.VMEM)
    smem = pl.BlockSpec(memory_space=pltpu.SMEM)
    out = jax.ShapeDtypeStruct((tokens, width), jnp.bfloat16)
    return pl.pallas_call(
        partial(out_kernel, step, sections),
        out_shape=(out, out),
        in_specs=[smem] + [vmem] * 4 + [anywhere] * (5 * sections),
        out_specs=(vmem, vmem),
        scratch_shapes=[
            pltpu.VMEM((4, width, channels), jnp.bfloat16),
            pltpu.SemaphoreType.DMA((4, 2)),
        ],
        compiler_params=pltpu.CompilerParams(vmem_limit_bytes=16 * MIB),
        cost_estimate=pl.CostEstimate(
            flops=16 * tokens * width * channels,
            bytes_accessed=8 * width * channels,
            transcendentals=0,
        ),
        name="project_out",
    )(plan, own_gated, core_gated, own_hidden, core_hidden, *[w for ws in weights for w in ws])


def taken_kernel(second, runs, plan, in_ref, out_ref, *refs):
    outs, sem = refs[:-1], refs[-1]
    section = 1 - plan[0] if second else plan[0]
    group = lax.axis_index("groups")
    part = outs[0].shape[0]
    mine = pl.ds(pl.multiple_of(group * part, part), part)
    pairs = [(out_ref.at[section, mine], outs[0])]
    for run, out in zip(runs, outs[1:]):
        for n, (p, q) in enumerate(run):
            pairs.append((in_ref.at[section, p, mine if q is None else pl.ds(q * part, part)], out.at[n]))
    copies = [pltpu.make_async_copy(*pair, sem.at[n]) for n, pair in enumerate(pairs)]
    for copy in copies[1:] + copies[:1]:
        copy.start()
    for copy in copies:
        copy.wait()


def taken(second, runs, plan, in_weights, out_weights):
    part, channels = out_weights.shape[1] // 2, out_weights.shape[2]
    far = pl.BlockSpec(memory_space=pltpu.HBM)
    near = pl.BlockSpec(memory_space=pltpu.VMEM)
    shapes = [(part, channels)] + [(len(run), part, channels) for run in runs]
    return pl.pallas_call(
        partial(taken_kernel, second, runs),
        out_shape=tuple(jax.ShapeDtypeStruct(shape, jnp.bfloat16) for shape in shapes),
        in_specs=[pl.BlockSpec(memory_space=pltpu.SMEM), far, far],
        out_specs=(near,) * len(shapes),
        scratch_shapes=[pltpu.SemaphoreType.DMA((5,))],
        compiler_params=pltpu.CompilerParams(vmem_limit_bytes=(8 if second else 56) * MIB),
        name="taken",
    )(plan, in_weights, out_weights)


def after(value, *others):
    return lax.optimization_barrier((value,) + others)[0]


EVERY = ("groups", "ctx", "chan")
PLANE = ("ctx", "chan")


class Rounds:
    def __init__(self):
        self.before, self.now = [], []

    def __call__(self, value, axes, pairs):
        return self.join(after(value, *self.before) if self.before else value, axes, pairs)

    def join(self, value, axes, pairs):
        self.now.append(lax.ppermute(value, axes, pairs))
        return self.now[-1]

    def turn(self):
        self.before, self.now = self.now, []


def holder(x, j):
    return 2 * x + j % 2


def keeper(x, j):
    return 3 * x


def other_keeper(x, j):
    return 2 - x


def plane_pairs(source, target):
    return [(flat(source(x, j), j), flat(target(x, j), j)) for x in range(2) for j in range(4)]


def group_pairs(source, target):
    return [
        (flat(source(x, j), j, q), flat(target(x, j), j, 1 - q))
        for x in range(2)
        for j in range(4)
        for q in range(2)
    ]


CORES = ctx_pairs(1)
CHIPS = ctx_pairs(2)
GROUPS = [(0, 1), (1, 0)]
ALONG = {
    k: [(flat(holder(x, j), (j - k) % 4), flat(holder(x, j), j)) for x in range(2) for j in range(4)]
    for k in (1, 2, 3)
}
TO_KEEPER = [pair for pair in plane_pairs(holder, keeper) if pair[0] != pair[1]]
TO_OTHER_KEEPER = plane_pairs(holder, other_keeper)
TO_KEEPER_OVER = group_pairs(holder, keeper)
OTHER_KEEPERS_OVER = group_pairs(other_keeper, other_keeper)
BESIDE = [(s, s ^ 1) for s in range(4)]
HALO = [(0, 1), (1, 2), (2, 3)]


def around(k):
    return [(s, (s + k) % 4) for s in range(4)]


def shards(stream, in_weights, out_weights, short_taps, medium_taps, plan):
    g, i, j = lax.axis_index("groups"), lax.axis_index("ctx"), lax.axis_index("chan")
    x, c, h = i // 2, i % 2, j % 2
    reach = medium_taps.shape[0]
    width = stream.shape[1]
    part = width // 2
    in_weights = in_weights.transpose(0, 2, 1, 3)
    near = (j // 2) == c
    send = Rounds()

    whole = lax.all_gather(stream, "chan", axis=1, tiled=True)
    runs = (((1, None), (2, None)), ((0, None),))
    out_a, kv_a, q_a = taken(False, runs, plan, in_weights, out_weights)
    x_kv = send(kv_a, "ctx", CHIPS)
    x_q = lax.ppermute(q_a, "ctx", CHIPS)
    core_in = send(after(in_weights, kv_a), "ctx", CORES)
    runs = (((1, None), (2, None)), ((0, 0), (0, 1)))
    out_b, kv_b, q_b = taken(True, runs, after(plan, kv_a), in_weights, out_weights)
    bands = tap_bands(after(medium_taps, kv_a))
    send.now += [out_b, bands]

    send.turn()
    y_kv = send(x_kv, "groups", GROUPS)
    x_kv_b = send(kv_b, "ctx", CHIPS)
    shard_a = [out_a] + [send(out_a, PLANE, ALONG[k]) for k in (1, 2, 3)]
    y_q = send(x_q, "groups", GROUPS)
    send.now.append(whole)
    c_x = lax.ppermute(jnp.concatenate([x_q, x_kv]), "ctx", CORES)

    send.turn()
    shard_a = jnp.stack(shard_a)
    cross_a = send(shard_a, PLANE, TO_OTHER_KEEPER)
    same_y = send(shard_a, EVERY, TO_KEEPER_OVER)
    c_y = send(jnp.concatenate([y_q, y_kv]), "ctx", CORES)
    same_a = send(shard_a, PLANE, TO_KEEPER)
    shard_b = [out_b] + [send(after(out_b, c_y, same_a), PLANE, ALONG[k]) for k in (1, 2, 3)]

    send.turn()
    shard_b = jnp.stack(shard_b)
    cross_y = send.join(cross_a, EVERY, OTHER_KEEPERS_OVER)
    weights_in = [[x_kv, y_kv, x_q, y_q, c_x, c_y]]
    weights_out = [[shard_a, same_a, same_y, cross_a, cross_y]]

    own_hidden = lax.dynamic_slice_in_dim(whole, (2 * c + h) * width, width, 1)
    to_core = lax.dynamic_slice_in_dim(whole, (2 * (1 - c) + h) * width, width, 1)
    core_hidden = lax.ppermute(to_core, "ctx", CORES)
    inputs = in_weights, core_in

    for step in range(STEPS):
        count = 1 if step == 0 else 2
        if step == 0:
            query, mixed = project_in("whole", step, plan, [whole], [], *inputs, weights_in)
        else:
            part_sums = project_in("first", step, plan, near_pieces, [], *inputs, weights_in)
            query, mixed = project_in("last", step, plan, far_pieces, part_sums, *inputs, weights_in)
        halo = lax.ppermute(mixed[-reach:], "ctx", HALO)
        if step == 0:
            c_kv_b = lax.ppermute(after(x_kv_b, halo), "ctx", CORES)
        gated = filter_and_gate(step, plan, halo, mixed, query, bands, short_taps)
        if step == 0:
            cross_b = send(after(shard_b, halo), PLANE, TO_OTHER_KEEPER)
        g_2, g_3, g_1 = (send.join(gated, "chan", around(k)) for k in (2, 3, 1))
        if step == 0:
            send.turn()
            y_kv_b = send.join(after(x_kv_b, cross_y), "groups", GROUPS)
            x_q_b = send(q_b, "ctx", CHIPS)
            same_b_y = lax.ppermute(after(shard_b, *send.before), EVERY, TO_KEEPER_OVER)
        own_gated = jnp.stack([gated, g_1, g_2, g_3])
        core_gated = lax.ppermute(own_gated, "ctx", CORES)
        own_hidden, core_hidden = project_out(
            step, plan, own_gated, core_gated, own_hidden, core_hidden, weights_out[:count]
        )
        swapped = lax.ppermute(core_hidden, "ctx", CORES)
        if step == STEPS - 1:
            return jnp.where((j // 2) == c, own_hidden, swapped)
        near_pieces = [own_hidden, swapped]
        beside_core = send.join(core_hidden, "chan", BESIDE)
        far_pieces = [send.join(own_hidden, "chan", BESIDE), lax.ppermute(beside_core, "ctx", CORES)]
        if step == 0:
            send.turn()
            both_b = send(jnp.concatenate([x_q_b, y_kv_b]), "ctx", CORES)
            same_b = send(shard_b, PLANE, TO_KEEPER)
            cross_b_y = send(cross_b, EVERY, OTHER_KEEPERS_OVER)
            weights_in.append([x_kv_b, y_kv_b, x_q_b, both_b, c_kv_b])
            weights_out.append([shard_b, same_b, same_b_y, cross_b, cross_b_y])


def solution(mesh):
    special = dict(mesh.shape) == {"groups": 2, "ctx": 4, "chan": 4}
    return jax.shard_map(
        shards if special else general_shards,
        mesh=mesh,
        in_specs=(
            P(("groups", "ctx"), "chan"),
            P(None, "ctx", None, "chan"),
            P(None, "ctx", "chan"),
            P(None, "chan"),
            P(None, "chan"),
            P(),
        ),
        out_specs=P(("groups", "ctx"), "chan"),
        check_vma=False,
    )
```

```python
from functools import partial

import jax
import jax.numpy as jnp
from jax import lax
from jax.experimental import pallas as pl
from jax.experimental.pallas import tpu as pltpu
from jax.sharding import PartitionSpec as P

STEPS = 4
MIB = 1024 * 1024


def passed_along(value, axis, steps):
    count = lax.axis_size(axis)
    leading, last = (max(0, -steps), min(count, count - steps))
    return lax.ppermute(value, axis, [(source, source + steps) for source in range(leading, last)])


def section_taps(section, short_taps, medium_taps):
    reach = medium_taps.shape[0]
    channels = short_taps.shape[1]
    padding = jnp.zeros((reach - short_taps.shape[0], channels), short_taps.dtype)
    short_full = jnp.concatenate([short_taps, padding], 0)
    group_size = channels // medium_taps.shape[1]
    medium_full = jnp.broadcast_to(
        medium_taps[:, :, None], (reach, medium_taps.shape[1], group_size)
    ).reshape(reach, channels)
    return jnp.where(section == 0, short_full, medium_full)


def causal_filter(extended, filter_taps):
    filtered = lax.conv_general_dilated(
        extended[None],
        filter_taps[::-1][:, None, :],
        (1,),
        "VALID",
        dimension_numbers=("NWC", "WIO", "NWC"),
        feature_group_count=filter_taps.shape[1],
        preferred_element_type=jnp.float32,
    )
    return filtered[0]


def filter_gate(projected, section, short_taps, medium_taps):
    query_bf = projected[:, 0].astype(jnp.bfloat16)
    mixed_bf = (projected[:, 1] * projected[:, 2]).astype(jnp.bfloat16)
    reach = medium_taps.shape[0]
    earlier = passed_along(mixed_bf[-reach:], "ctx", 1)
    extended = jnp.concatenate([earlier[1:], mixed_bf], 0)
    filtered = causal_filter(extended, section_taps(section, short_taps, medium_taps))
    return (query_bf.astype(jnp.float32) * filtered).astype(jnp.bfloat16)


def general_shards(stream, in_weights, out_weights, short_taps, medium_taps, plan):
    hidden = stream
    weights_in = lax.all_gather(in_weights, "ctx", axis=1, tiled=True)
    weights_out = lax.all_gather(out_weights, "ctx", axis=1, tiled=True)
    for step in range(STEPS):
        section = plan[step]
        full_rows = lax.all_gather(hidden, "chan", axis=1, tiled=True)
        widened = full_rows.astype(jnp.float32)
        row_scale = lax.rsqrt(jnp.mean(widened * widened, axis=1, keepdims=True) + 1e-05)
        chosen = lax.dynamic_index_in_dim(weights_in, section, 0, keepdims=False)
        projected = jnp.dot(
            full_rows, chosen.reshape(chosen.shape[0], -1), preferred_element_type=jnp.float32
        )
        projected = projected.reshape(full_rows.shape[0], 3, -1) * row_scale[:, :, None]
        gated = filter_gate(projected, section, short_taps, medium_taps)
        chosen = lax.dynamic_index_in_dim(weights_out, section, 0, keepdims=False)
        product = lax.dot_general(
            gated, chosen, (((1,), (1,)), ((), ())), preferred_element_type=jnp.float32
        )
        update = lax.psum_scatter(
            product.astype(jnp.bfloat16), "chan", scatter_dimension=1, tiled=True
        ).astype(jnp.float32)
        hidden = (hidden.astype(jnp.float32) + update).astype(jnp.bfloat16)
    return hidden


SECOND, GROUP, SAME, MATCH, ROW = range(5)


def scalars(plan, step):
    g, i, j = lax.axis_index("groups"), lax.axis_index("ctx"), lax.axis_index("chan")
    x, c, h = i >> 1, i & 1, j & 1
    second = (plan[step] != plan[0]).astype(jnp.int32)
    same, match = (x == c).astype(jnp.int32), (c == h).astype(jnp.int32)
    return [second, g, same, match, i, i ^ 1, i ^ 2, i ^ 3]


def ctx_pairs(change):
    return [(i, i ^ change) for i in range(4)]


def flat(i, j, g=None):
    return (i * 4 + j) if g is None else (g * 16 + i * 4 + j)


OWN, CORE, CHIP, BOTH = range(4)


def in_kernel(mode, step, sections, plan, *refs):
    meta = scalars(plan, step)
    section = plan[step]
    count = 1 if mode == "whole" else 2
    pieces, refs = refs[:count], refs[count:]
    if mode == "last":
        earlier, earlier_square, refs = refs[0], refs[1], refs[2:]
    own_in, core_in = refs[:2]
    weights, refs = [refs[2:8], refs[8:13]], refs[8 if sections == 1 else 13 :]
    out_ref, out_ref2, hidden, held, total, held_sem = refs
    tokens, width = hidden.shape[1:]
    part = width // 2
    group = meta[GROUP]
    slots = held.shape[1]

    def span(q):
        return pl.ds(pl.multiple_of(q * part, part), part)

    def start(kind, p, slot, sources):
        if kind in (OWN, CORE):
            source = own_in if kind == OWN else core_in
            halves = [(source.at[section, p, span(q)], span(q)) for q in range(2)]
        elif len(sources) == 6:
            if kind == BOTH:
                mine, other, at = sources[4], sources[5], p
            else:
                mine, other, at = (sources[2], sources[3], 0) if p == 0 else (sources[0], sources[1], p - 1)
            halves = [(mine.at[at], span(group)), (other.at[at], span(1 - group))]
        elif p == 0:
            source = sources[2 if kind == CHIP else 3]
            halves = [(source.at[q], span(q)) for q in range(2)]
        else:
            mine, other, at = (sources[0], sources[1], p - 1) if kind == CHIP else (sources[4], sources[3], p + 1)
            halves = [(mine.at[p - 1], span(group)), (other.at[at], span(1 - group))]
        for q in range(2):
            pltpu.make_async_copy(
                halves[q][0], held.at[p, slot, halves[q][1]], held_sem.at[p, slot, q]
            ).start()

    def start_kinds(kinds, sources):
        for p in (1, 2, 0):
            for slot, kind in enumerate(kinds):
                start(kind, p, slot, sources)

    if mode == "whole":
        start_kinds((OWN, CORE, CHIP, BOTH), weights[0])
    else:
        for match in range(2):
            kinds = (OWN, CHIP) if match == (mode == "first") else (CORE, BOTH)
            for s in range(sections):
                here = jnp.logical_and(meta[MATCH] == match, meta[SECOND] == s)
                pl.when(here)(partial(start_kinds, kinds, weights[s]))

    square = jnp.zeros((tokens, 1), jnp.float32)
    for k in range(slots):
        if mode == "whole":
            piece = pieces[0][:, k * width : (k + 1) * width]
            hidden[k] = piece
        else:
            piece = pieces[k][...]
            hidden[1 - meta[SAME] if k == 0 else meta[SAME]] = piece
        wide = piece.astype(jnp.float32)
        square = square + jnp.sum(wide * wide, axis=1, keepdims=True)
    if mode == "last":
        square = square + earlier_square[:, :1]
    if mode == "first":
        out_ref2[...] = jnp.broadcast_to(square, out_ref2.shape)
    else:
        scale = lax.rsqrt(square / (4 * width) + 1e-05)

    for p in (1, 2, 0):
        for slot in range(slots):
            for q in range(2):
                pltpu.make_async_copy(
                    own_in.at[0, 0, pl.ds(0, part)],
                    held.at[p, slot, pl.ds(0, part)],
                    held_sem.at[p, slot, q],
                ).wait()
            at = meta[ROW + slot] if mode == "whole" else slot
            product = jnp.dot(hidden[at], held[p, slot], preferred_element_type=jnp.float32)
            if slot > 0:
                total[p] += product
            elif mode == "last":
                total[p] = earlier[p] + product
            else:
                total[p] = product
    if mode == "first":
        out_ref[...] = total[...]
    else:
        out_ref[...] = (total[0] * scale).astype(out_ref.dtype)
        out_ref2[...] = ((total[1] * scale) * (total[2] * scale)).astype(out_ref2.dtype)


def project_in(mode, step, plan, pieces, earlier, own_in, core_in, weights):
    width, channels = own_in.shape[2:]
    tokens = pieces[0].shape[0]
    sections = len(weights)
    slots = 4 if mode == "whole" else 2
    anywhere = pl.BlockSpec(memory_space=pl.ANY)
    vmem = pl.BlockSpec(memory_space=pltpu.VMEM)
    smem = pl.BlockSpec(memory_space=pltpu.SMEM)
    if mode == "first":
        out = (
            jax.ShapeDtypeStruct((3, tokens, channels), jnp.float32),
            jax.ShapeDtypeStruct((tokens, 128), jnp.float32),
        )
    else:
        out = (jax.ShapeDtypeStruct((tokens, channels), jnp.bfloat16),) * 2
    return pl.pallas_call(
        partial(in_kernel, mode, step, sections),
        out_shape=out,
        in_specs=[smem]
        + [vmem] * (len(pieces) + len(earlier))
        + [anywhere] * (2 + sum(len(w) for w in weights)),
        out_specs=(vmem, vmem),
        scratch_shapes=[
            pltpu.VMEM((slots, tokens, width), jnp.bfloat16),
            pltpu.VMEM((3, slots, width, channels), jnp.bfloat16),
            pltpu.VMEM((3, tokens, channels), jnp.float32),
            pltpu.SemaphoreType.DMA((3, slots, 2)),
        ],
        compiler_params=pltpu.CompilerParams(vmem_limit_bytes=44 * MIB),
        cost_estimate=pl.CostEstimate(
            flops=6 * slots * tokens * width * channels,
            bytes_accessed=6 * slots * width * channels,
            transcendentals=0,
        ),
        name="project_in_" + mode,
    )(plan, *pieces, *earlier, own_in, core_in, *[w for ws in weights for w in ws])


BLOCK = 64


def filter_kernel(step, plan, halo, mixed, query, bands, short, gated, extended):
    reach, tokens = halo.shape[0], mixed.shape[0]
    channels = mixed.shape[1]
    group_size = channels // (bands.shape[0] // BLOCK)

    @pl.when(plan[step] == 0)
    def _():
        extended[:reach] = halo[...].astype(jnp.float32)
        extended[reach:] = mixed[...].astype(jnp.float32)
        taps = short[...].astype(jnp.float32)
        total = jnp.zeros((tokens, channels), jnp.float32)
        for t in range(taps.shape[0]):
            total = total + taps[t : t + 1] * extended[reach - t : reach - t + tokens]
        gated[...] = (query[...].astype(jnp.float32) * total).astype(gated.dtype)

    @pl.when(plan[step] != 0)
    def _():
        lanes = 128
        per_tile = lanes // group_size
        lane_group = lax.broadcasted_iota(jnp.int32, (BLOCK, lanes), 1) // group_size
        for tile in range(channels // lanes):
            at = slice(tile * lanes, (tile + 1) * lanes)
            column = jnp.concatenate([halo[:, at], mixed[:, at]], 0)
            band = bands[tile * per_tile * BLOCK : (tile + 1) * per_tile * BLOCK]
            for b in range(tokens // BLOCK):
                window = column[b * BLOCK : b * BLOCK + reach + BLOCK]
                product = jnp.dot(band, window, preferred_element_type=jnp.float32)
                total = product[:BLOCK]
                for m in range(1, per_tile):
                    total = jnp.where(
                        lane_group == m, product[m * BLOCK : (m + 1) * BLOCK], total
                    )
                rows = slice(b * BLOCK, (b + 1) * BLOCK)
                gated[rows, at] = (query[rows, at].astype(jnp.float32) * total).astype(gated.dtype)


def filter_and_gate(step, plan, halo, mixed, query, bands, short):
    tokens, channels = mixed.shape
    vmem = pl.BlockSpec(memory_space=pltpu.VMEM)
    return pl.pallas_call(
        partial(filter_kernel, step),
        out_shape=jax.ShapeDtypeStruct(mixed.shape, jnp.bfloat16),
        in_specs=[pl.BlockSpec(memory_space=pltpu.SMEM)] + [vmem] * 5,
        out_specs=vmem,
        scratch_shapes=[pltpu.VMEM((halo.shape[0] + tokens, channels), jnp.float32)],
        compiler_params=pltpu.CompilerParams(vmem_limit_bytes=8 * MIB),
        cost_estimate=pl.CostEstimate(
            flops=2 * tokens * channels * 1024, bytes_accessed=8 * tokens * channels, transcendentals=0
        ),
        name="filter_and_gate",
    )(plan, halo, mixed, query, bands, short)


def tap_bands(medium_taps):
    reach, groups = medium_taps.shape
    length = 2 * reach
    zero = jnp.zeros((groups, 1), medium_taps.dtype)
    tail = jnp.zeros((groups, reach - 1), medium_taps.dtype)
    cycle = jnp.concatenate([zero, medium_taps[::-1].T, tail], 1)
    skewed = jnp.broadcast_to(cycle[:, None], (groups, BLOCK, length)).reshape(groups, -1)
    skewed = skewed[:, : BLOCK * (length - 1)].reshape(groups, BLOCK, length - 1)
    return skewed[:, :, : reach + BLOCK].reshape(groups * BLOCK, reach + BLOCK)


def out_kernel(step, sections, plan, *refs):
    meta = scalars(plan, step)
    own_gated, core_gated, own_hidden, core_hidden = refs[:4]
    weights = [refs[4 + 5 * s : 9 + 5 * s] for s in range(sections)]
    own_out, core_out, held, held_sem = refs[4 + 5 * sections :]
    tokens, width = own_hidden.shape
    part = width // 2
    group = meta[GROUP]
    mine = pl.ds(pl.multiple_of(group * part, part), part)
    other = pl.ds(pl.multiple_of((1 - group) * part, part), part)

    def start(first, second):
        for k in range(4):
            pltpu.make_async_copy(first.at[k], held.at[k, mine], held_sem.at[k, 0]).start()
            pltpu.make_async_copy(second.at[k], held.at[k, other], held_sem.at[k, 1]).start()

    for s in range(sections):
        shard, same_mine, same_other, cross_mine, cross_other = weights[s]
        cases = (
            (meta[SAME] == 0, cross_mine, cross_other),
            (meta[SAME] + meta[MATCH] == 2, shard, same_other),
            (meta[SAME] - meta[MATCH] == 1, same_mine, same_other),
        )
        for here, first, second in cases:
            if sections > 1:
                here = jnp.logical_and(here, meta[SECOND] == s)
            pl.when(here)(partial(start, first, second))

    total = None
    for k in range(4):
        for n, at in enumerate((mine, other)):
            pltpu.make_async_copy(weights[0][0].at[0], held.at[k, at], held_sem.at[k, n]).wait()
        both = jnp.concatenate([own_gated[k], core_gated[k]], 0)
        product = lax.dot_general(
            both, held[k], (((1,), (1,)), ((), ())), preferred_element_type=jnp.float32
        )
        total = product if total is None else total + product
    own_out[...] = (own_hidden[...].astype(jnp.float32) + total[:tokens]).astype(own_out.dtype)
    core_out[...] = (core_hidden[...].astype(jnp.float32) + total[tokens:]).astype(core_out.dtype)


def project_out(step, plan, own_gated, core_gated, own_hidden, core_hidden, weights):
    tokens, width = own_hidden.shape
    channels = own_gated.shape[2]
    sections = len(weights)
    anywhere = pl.BlockSpec(memory_space=pl.ANY)
    vmem = pl.BlockSpec(memory_space=pltpu.VMEM)
    smem = pl.BlockSpec(memory_space=pltpu.SMEM)
    out = jax.ShapeDtypeStruct((tokens, width), jnp.bfloat16)
    return pl.pallas_call(
        partial(out_kernel, step, sections),
        out_shape=(out, out),
        in_specs=[smem] + [vmem] * 4 + [anywhere] * (5 * sections),
        out_specs=(vmem, vmem),
        scratch_shapes=[
            pltpu.VMEM((4, width, channels), jnp.bfloat16),
            pltpu.SemaphoreType.DMA((4, 2)),
        ],
        compiler_params=pltpu.CompilerParams(vmem_limit_bytes=(44 if sections == 1 else 16) * MIB),
        cost_estimate=pl.CostEstimate(
            flops=16 * tokens * width * channels,
            bytes_accessed=8 * width * channels,
            transcendentals=0,
        ),
        name="project_out",
    )(plan, own_gated, core_gated, own_hidden, core_hidden, *[w for ws in weights for w in ws])


def taken_kernel(second, runs, plan, in_ref, out_ref, *refs):
    outs, sem = refs[:-1], refs[-1]
    section = 1 - plan[0] if second else plan[0]
    group = lax.axis_index("groups")
    part = outs[0].shape[0]
    mine = pl.ds(pl.multiple_of(group * part, part), part)
    pairs = [(out_ref.at[section, mine], outs[0])]
    for run, out in zip(runs, outs[1:]):
        for n, (p, q) in enumerate(run):
            pairs.append((in_ref.at[section, p, mine if q is None else pl.ds(q * part, part)], out.at[n]))
    copies = [pltpu.make_async_copy(*pair, sem.at[n]) for n, pair in enumerate(pairs)]
    for copy in copies[1:] + copies[:1]:
        copy.start()
    for copy in copies:
        copy.wait()


def taken(second, runs, plan, in_weights, out_weights):
    part, channels = out_weights.shape[1] // 2, out_weights.shape[2]
    far = pl.BlockSpec(memory_space=pltpu.HBM)
    near = pl.BlockSpec(memory_space=pltpu.VMEM)
    shapes = [(part, channels)] + [(len(run), part, channels) for run in runs]
    return pl.pallas_call(
        partial(taken_kernel, second, runs),
        out_shape=tuple(jax.ShapeDtypeStruct(shape, jnp.bfloat16) for shape in shapes),
        in_specs=[pl.BlockSpec(memory_space=pltpu.SMEM), far, far],
        out_specs=(near,) * len(shapes),
        scratch_shapes=[pltpu.SemaphoreType.DMA((5,))],
        compiler_params=pltpu.CompilerParams(vmem_limit_bytes=(8 if second else 56) * MIB),
        name="taken",
    )(plan, in_weights, out_weights)


def after(value, *others):
    return lax.optimization_barrier((value,) + others)[0]


EVERY = ("groups", "ctx", "chan")
PLANE = ("ctx", "chan")


class Rounds:
    def __init__(self):
        self.before, self.now = [], []

    def __call__(self, value, axes, pairs):
        return self.join(after(value, *self.before) if self.before else value, axes, pairs)

    def join(self, value, axes, pairs):
        self.now.append(lax.ppermute(value, axes, pairs))
        return self.now[-1]

    def turn(self):
        self.before, self.now = self.now, []


def holder(x, j):
    return 2 * x + j % 2


def keeper(x, j):
    return 3 * x


def other_keeper(x, j):
    return 2 - x


def plane_pairs(source, target):
    return [(flat(source(x, j), j), flat(target(x, j), j)) for x in range(2) for j in range(4)]


def group_pairs(source, target):
    return [
        (flat(source(x, j), j, q), flat(target(x, j), j, 1 - q))
        for x in range(2)
        for j in range(4)
        for q in range(2)
    ]


CORES = ctx_pairs(1)
CHIPS = ctx_pairs(2)
GROUPS = [(0, 1), (1, 0)]
ALONG = {
    k: [(flat(holder(x, j), (j - k) % 4), flat(holder(x, j), j)) for x in range(2) for j in range(4)]
    for k in (1, 2, 3)
}
TO_KEEPER = [pair for pair in plane_pairs(holder, keeper) if pair[0] != pair[1]]
TO_OTHER_KEEPER = plane_pairs(holder, other_keeper)
TO_KEEPER_OVER = group_pairs(holder, keeper)
OTHER_KEEPERS_OVER = group_pairs(other_keeper, other_keeper)
BESIDE = [(s, s ^ 1) for s in range(4)]
HALO = [(0, 1), (1, 2), (2, 3)]


def around(k):
    return [(s, (s + k) % 4) for s in range(4)]


def shards(stream, in_weights, out_weights, short_taps, medium_taps, plan):
    g, i, j = lax.axis_index("groups"), lax.axis_index("ctx"), lax.axis_index("chan")
    x, c, h = i // 2, i % 2, j % 2
    reach = medium_taps.shape[0]
    width = stream.shape[1]
    part = width // 2
    in_weights = in_weights.transpose(0, 2, 1, 3)
    near = (j // 2) == c
    send = Rounds()

    whole = lax.all_gather(stream, "chan", axis=1, tiled=True)
    runs = (((1, None), (2, None)), ((0, None),))
    out_a, kv_a, q_a = taken(False, runs, plan, in_weights, out_weights)
    x_kv = send(kv_a, "ctx", CHIPS)
    x_q = lax.ppermute(q_a, "ctx", CHIPS)
    core_in = send(after(in_weights, kv_a), "ctx", CORES)
    runs = (((1, None), (2, None)), ((0, 0), (0, 1)))
    out_b, kv_b, q_b = taken(True, runs, after(plan, kv_a), in_weights, out_weights)
    bands = tap_bands(after(medium_taps, kv_a))
    send.now += [out_b, bands]

    send.turn()
    y_kv = send(x_kv, "groups", GROUPS)
    x_kv_b = send(kv_b, "ctx", CHIPS)
    shard_a = [out_a] + [send(out_a, PLANE, ALONG[k]) for k in (1, 2, 3)]
    y_q = send(x_q, "groups", GROUPS)
    send.now.append(whole)
    c_x = lax.ppermute(jnp.concatenate([x_q, x_kv]), "ctx", CORES)

    send.turn()
    shard_a = jnp.stack(shard_a)
    cross_a = send(shard_a, PLANE, TO_OTHER_KEEPER)
    same_y = send(shard_a, EVERY, TO_KEEPER_OVER)
    c_y = send(jnp.concatenate([y_q, y_kv]), "ctx", CORES)
    same_a = send(shard_a, PLANE, TO_KEEPER)
    shard_b = [out_b] + [send(after(out_b, c_y, same_a), PLANE, ALONG[k]) for k in (1, 2, 3)]

    send.turn()
    shard_b = jnp.stack(shard_b)
    cross_y = send.join(cross_a, EVERY, OTHER_KEEPERS_OVER)
    weights_in = [[x_kv, y_kv, x_q, y_q, c_x, c_y]]
    weights_out = [[shard_a, same_a, same_y, cross_a, cross_y]]

    own_hidden = lax.dynamic_slice_in_dim(whole, (2 * c + h) * width, width, 1)
    to_core = lax.dynamic_slice_in_dim(whole, (2 * (1 - c) + h) * width, width, 1)
    core_hidden = lax.ppermute(to_core, "ctx", CORES)
    inputs = in_weights, core_in

    for step in range(STEPS):
        count = 1 if step == 0 else 2
        if step == 0:
            query, mixed = project_in("whole", step, plan, [whole], [], *inputs, weights_in)
        else:
            part_sums = project_in("first", step, plan, near_pieces, [], *inputs, weights_in)
            query, mixed = project_in("last", step, plan, far_pieces, part_sums, *inputs, weights_in)
        halo = lax.ppermute(mixed[-reach:], "ctx", HALO)
        if step == 0:
            c_kv_b = lax.ppermute(after(x_kv_b, halo), "ctx", CORES)
        gated = filter_and_gate(step, plan, halo, mixed, query, bands, short_taps)
        if step == 0:
            cross_b = send(after(shard_b, halo), PLANE, TO_OTHER_KEEPER)
        g_2, g_3, g_1 = (send.join(gated, "chan", around(k)) for k in (2, 3, 1))
        if step == 0:
            send.turn()
            y_kv_b = send.join(after(x_kv_b, cross_y), "groups", GROUPS)
            x_q_b = send(q_b, "ctx", CHIPS)
            same_b_y = lax.ppermute(after(shard_b, *send.before), EVERY, TO_KEEPER_OVER)
        own_gated = jnp.stack([gated, g_1, g_2, g_3])
        core_gated = lax.ppermute(own_gated, "ctx", CORES)
        own_hidden, core_hidden = project_out(
            step, plan, own_gated, core_gated, own_hidden, core_hidden, weights_out[:count]
        )
        swapped = lax.ppermute(core_hidden, "ctx", CORES)
        if step == STEPS - 1:
            return jnp.where((j // 2) == c, own_hidden, swapped)
        near_pieces = [own_hidden, swapped]
        beside_core = send.join(core_hidden, "chan", BESIDE)
        far_pieces = [send.join(own_hidden, "chan", BESIDE), lax.ppermute(beside_core, "ctx", CORES)]
        if step == 0:
            send.turn()
            both_b = send(jnp.concatenate([x_q_b, y_kv_b]), "ctx", CORES)
            same_b = send(shard_b, PLANE, TO_KEEPER)
            cross_b_y = send(cross_b, EVERY, OTHER_KEEPERS_OVER)
            weights_in.append([x_kv_b, y_kv_b, x_q_b, both_b, c_kv_b])
            weights_out.append([shard_b, same_b, same_b_y, cross_b, cross_b_y])


def solution(mesh):
    special = dict(mesh.shape) == {"groups": 2, "ctx": 4, "chan": 4}
    return jax.shard_map(
        shards if special else general_shards,
        mesh=mesh,
        in_specs=(
            P(("groups", "ctx"), "chan"),
            P(None, "ctx", None, "chan"),
            P(None, "ctx", "chan"),
            P(None, "chan"),
            P(None, "chan"),
            P(),
        ),
        out_specs=P(("groups", "ctx"), "chan"),
        check_vma=False,
    )
```
